256 devices in a mesh: wide: 32 (over y, z_hi, core), narrow: 8 (over x, z_lo).
Axes of the slice: x: 4, y: 4, z: 8 (z_hi: 4, z_lo: 2; z = z_hi * 2 + z_lo), core: 2. Of those that a mesh axis runs over, the one named last changes fastest.
Arguments:
- activations: bfloat16 [64, 48, 64, 512], P('wide', 'narrow'), may hold values from -6 to 6
- conv_weight: bfloat16 [3, 3, 3, 512, 16], replicated, may hold values from -0.0546875 to 0.0546875
- patch_weight: bfloat16 [64, 3072], replicated, may hold values from -0.75 to 0.75
- patch_bias: float32 [3072], replicated, may hold values from -3 to 3
- shift: float32 [3072], replicated, may hold values from -3 to 3
- scale: float32 [3072], replicated, may hold values from -0.9 to 0.9
- qkv_weight: bfloat16 [3072, 3, 2048], P('wide', None, 'narrow'), may hold values from -0.109375 to 0.109375
- qkv_bias: float32 [3, 2048], P(None, 'narrow'), may hold values from -3 to 3
- norm_gains: float32 [2, 128], replicated, may hold values from 0.25 to 1.75
Outputs:
- qkv: bfloat16 [3, 49152, 2048], P(None, 'wide', 'narrow')
The draws below stay inside these ranges and needn't reach their ends.
All inputs are finite; a program needn't handle non-finite values.
Results may differ from the reference program's by a relative error of at most 0.0055.
Values may be sent and summed in bfloat16 or wider, within the bound.
A program may use at most 128 MiB of HBM per device.

```python
import jax
import jax.numpy as jnp
from jax import lax

COLS = 64
C = 512
LAT = 16
D = 3072
HEADS = 16
HD = 128
FRAMES = 64
ROWS = 48


def block_levels(rng, extent, shards, low, high):
    loudness = 1.0
    for axis_at, parts in shards:
        steps = jax.random.uniform(jax.random.fold_in(jax.random.fold_in(rng, 6), axis_at), (parts,), jnp.float32, low / len(shards), high / len(shards))
        loudness = loudness * jnp.repeat(jnp.exp(steps), extent[axis_at] // parts).reshape((-1,) + (1,) * (len(extent) - 1 - axis_at))
    return loudness


def bell_draw(key, shape, scale, bound, cuts=(), held_as=jnp.bfloat16):
    level = block_levels(key, shape, cuts, -0.22, 0.18) if cuts else 1.0
    entries = jax.random.normal(key, shape, jnp.float32) * scale * level
    return jnp.minimum(jnp.maximum(entries, -bound), bound).astype(held_as)


def setup_inputs(seed: int = 0) -> dict:
    splits = jax.random.split(jax.random.key(seed), 10)
    return {
        "activations": bell_draw(splits[0], (FRAMES, ROWS, COLS, C), 1.0, 6.0, ((0, 32), (1, 8))),
        "conv_weight": bell_draw(splits[1], (3, 3, 3, C, LAT), (27 * C) ** -0.5, 0.0546875),
        "patch_weight": bell_draw(splits[2], (4 * LAT, D), (4 * LAT) ** -0.5, 0.75),
        "patch_bias": bell_draw(splits[3], (D,), 0.5, 3.0, (), jnp.float32),
        "shift": bell_draw(splits[4], (D,), 0.5, 3.0, (), jnp.float32),
        "scale": bell_draw(splits[5], (D,), 0.3, 0.9, (), jnp.float32),
        "qkv_weight": bell_draw(splits[6], (D, 3, HEADS * HD), D ** -0.5, 0.109375, ((0, 32), (2, 8))),
        "qkv_bias": bell_draw(splits[7], (3, HEADS * HD), 0.5, 3.0, ((1, 8),), jnp.float32),
        "norm_gains": jnp.clip(1.0 + 0.15 * jax.random.normal(splits[8], (2, HD), jnp.float32), 0.25, 1.75),
    }


def spatial_sums(products, row_count, col_count):
    result = []
    for time_tap in range(3):
        total = jnp.zeros(products.shape[:1] + (row_count, col_count, products.shape[-1]), jnp.float32)
        for row_tap in range(3):
            for col_tap in range(3):
                total = total + products[:, row_tap:row_tap + row_count, col_tap:col_tap + col_count, time_tap, row_tap, col_tap, :]
        result.append(total)
    return result

def embed(patches, patch_weight, patch_bias, shift, scale):
    embedded = jnp.dot(patches, patch_weight, preferred_element_type=jnp.float32) + patch_bias
    centre = embedded - lax.optimization_barrier(jnp.mean(embedded, axis=-1, keepdims=True))
    spread = lax.optimization_barrier(jnp.mean(centre * centre, axis=-1, keepdims=True))
    normed = centre * lax.rsqrt(spread + 1e-06)
    return (normed * (1.0 + scale) + shift).astype(jnp.bfloat16)

def head_norms(totals, qkv_bias, norm_gains, head_dim):
    token_count = totals.shape[0]
    biased = totals + qkv_bias.reshape(-1)
    split = biased.reshape(token_count, 3, -1, head_dim)

    def rms(values, gain):
        return values * lax.rsqrt(lax.optimization_barrier(jnp.mean(values * values, axis=-1, keepdims=True)) + 1e-06) * gain
    query = rms(split[:, 0], norm_gains[0])
    keys = rms(split[:, 1], norm_gains[1])
    stacked = jnp.stack([query, keys, split[:, 2]], axis=1)
    return stacked.reshape(token_count, 3, -1).astype(jnp.bfloat16)

def reference(activations, conv_weight, patch_weight, patch_bias, shift, scale, qkv_weight, qkv_bias, norm_gains):
    frame_count, row_count, col_count, channels = activations.shape
    lat_channels = conv_weight.shape[4]
    head_dim = norm_gains.shape[1]
    width = qkv_weight.shape[0]
    conv_matrix = jnp.transpose(conv_weight, (3, 0, 1, 2, 4)).reshape(channels, 27 * lat_channels)
    acted = jax.nn.silu(activations.astype(jnp.float32)).astype(jnp.bfloat16)
    padded = jnp.concatenate([acted[:1], acted[:1], acted], axis=0)
    padded = jnp.pad(padded, ((0, 0), (1, 1), (1, 1), (0, 0)))

    def per_frame(frame):
        products = jnp.dot(frame.reshape(-1, channels), conv_matrix, preferred_element_type=jnp.float32)
        products = products.reshape(1, row_count + 2, col_count + 2, 3, 3, 3, lat_channels)
        return jnp.stack([piece[0] for piece in spatial_sums(products, row_count, col_count)], axis=0)
    sums = lax.map(per_frame, padded)
    latents = (sums[2:, 2] + sums[1:-1, 1] + sums[:-2, 0]).astype(jnp.bfloat16)
    patches = latents.reshape(frame_count, row_count // 2, 2, col_count // 2, 2, lat_channels)
    patches = jnp.transpose(patches, (0, 1, 3, 2, 4, 5)).reshape(frame_count, -1, 4 * lat_channels)
    weight_flat = qkv_weight.reshape(width, -1)

    def per_block(block):
        features = embed(block, patch_weight, patch_bias, shift, scale)
        totals = jnp.dot(features, weight_flat, preferred_element_type=jnp.float32)
        return head_norms(totals, qkv_bias, norm_gains, head_dim)
    outputs = lax.map(per_block, patches)
    outputs = outputs.reshape(-1, 3, outputs.shape[-1])
    return jnp.transpose(outputs, (1, 0, 2))
```

```python
import functools

import jax
import jax.numpy as jnp
from jax import lax
from jax.experimental import pallas as pl
from jax.experimental.pallas import tpu as pltpu
from jax.sharding import PartitionSpec as P

MESH = pl.DeviceIdType.MESH
F32 = jnp.float32
BF16 = jnp.bfloat16
CORES = 2
DEPTHS = 4
LANES = 128


def rolled(x, by):
    return pltpu.roll(x, by % x.shape[1], 1)


def halves(x):
    high = x.astype(BF16)
    return high, (x - high.astype(F32)).astype(BF16)


def dot(a, b):
    return lax.dot_general(a, b, (((1,), (0,)), ((), ())), preferred_element_type=F32)


def dot_t(a, b):
    return lax.dot_general(a, b, (((1,), (1,)), ((), ())), preferred_element_type=F32)


def front(
    sizes,
    act, cw, pw, pb, sh, sc, qw,
    x_out, r_out, m_out, e_out,
    act_v, cw_v, pw_v, pb_v, sh_v, sc_v, qw_v,
    part, got1, sum1, got2, own3, m_all, prod,
    a_v, b_v, at_v, ab_v, bm_v, bt_v, bb_v,
    wst, x_all, r_all,
    in_sem, act_sem, s1, g1, s2, g2, s3, g3, sx, gx, sr, gr, sh_sem, gh_sem,
):
    wides, narrows, rows, width = sizes
    span = qw.shape[1]
    w = lax.axis_index("wide")
    n = lax.axis_index("narrow")
    pairs = rows // 2
    group8 = wides // DEPTHS
    core = w % CORES
    depth = (w // CORES) % DEPTHS
    high = w // (CORES * DEPTHS)
    me8 = high * CORES + core

    def wide_of(q, z):
        return ((q // CORES) * DEPTHS + z) * CORES + q % CORES

    loads = []
    for k, (src, dst) in enumerate(
        [(pw, pw_v), (sc, sc_v), (sh, sh_v), (pb, pb_v), (qw, qw_v.at[:, pl.ds(0, span), :]), (cw, cw_v)]
    ):
        copy = pltpu.make_async_copy(src, dst, in_sem.at[k])
        copy.start()
        loads.append(copy)
    act_loads = []
    for k in range(pairs):
        for t in range(2):
            copy = pltpu.make_async_copy(
                act.at[t, pl.ds(2 * k, 2)], act_v.at[pl.ds(2 * k, 2), t], act_sem.at[2 * k + t]
            )
            copy.start()
            act_loads.append(copy)

    barrier = pltpu.get_barrier_semaphore()

    def greet(wide, narrow):
        pl.semaphore_signal(barrier, inc=1, device_id=(wide, narrow), device_id_type=MESH)

    for i in range(1, group8):
        greet(wide_of((me8 + i) % group8, depth), n)
    for i in range(1, DEPTHS):
        greet(wide_of(me8, (depth + i) % DEPTHS), n)
    for i in range(1, narrows):
        greet(w, (n + i) % narrows)
    has_next = w < wides - 1
    has_prev = w > 0
    for there, dw in ((has_next, 1), (has_prev, -1)):
        for dn in (-1, 0, 1):
            inside = there
            if dn == -1:
                inside = jnp.logical_and(there, n > 0)
            if dn == 1:
                inside = jnp.logical_and(there, n < narrows - 1)

            @pl.when(inside)
            def _():
                greet(w + dw, n + dn)

    sides = jnp.where(has_next, 1, 0) + jnp.where(has_prev, 1, 0)
    across = 1 + jnp.where(n > 0, 1, 0) + jnp.where(n < narrows - 1, 1, 0)
    expected = (group8 - 1) + (DEPTHS - 1) + (narrows - 1) + sides * across

    qw_v[:, span:, :] = jnp.zeros((3, qw_v.shape[1] - span, qw_v.shape[2]), BF16)
    for copy in loads[:5]:
        copy.wait()
    weight = pw_v[...].astype(F32)
    means = jnp.sum(weight, axis=1, keepdims=True) * (1.0 / width)
    bias_mean = jnp.sum(pb_v[...], axis=1, keepdims=True) * (1.0 / width)
    begin = w * span
    base = pl.multiple_of(jnp.minimum(begin // LANES, width // LANES - 2) * LANES, LANES)
    window = pl.ds(base, 2 * LANES)
    gain = 1.0 + sc_v[:, window]
    main = (pw_v[:, window].astype(F32) - means) * gain
    extra_b = (pb_v[:, window] - bias_mean) * gain
    extra_s = sh_v[:, window]
    pad = jnp.zeros((14, 2 * LANES), F32)
    stacked = jnp.concatenate([main, extra_b, extra_s, pad], axis=0)
    shift_by = (2 * LANES - (begin - base)) % (2 * LANES)
    stacked = pltpu.roll(stacked, shift_by, 1)[:, :LANES]
    lane = lax.broadcasted_iota(jnp.int32, stacked.shape, 1)
    stacked = jnp.where(lane < span, stacked, 0.0)
    top = stacked[:64]
    bottom = stacked[64:]
    row16 = lax.broadcasted_iota(jnp.int32, bottom.shape, 0)
    row_b = jnp.sum(jnp.where(row16 == 0, bottom, 0.0), axis=0, keepdims=True)
    row_s = jnp.sum(jnp.where(row16 == 1, bottom, 0.0), axis=0, keepdims=True)
    extras = jnp.zeros((8, qw.shape[2]), F32)
    for j in range(3):
        ext = jnp.where(row16 == 2 * j, row_b, jnp.where(row16 == 2 * j + 1, row_s, 0.0))
        hi, lo = halves(jnp.concatenate([top, ext], axis=0))
        res = dot(hi, qw_v[j]) + dot(lo, qw_v[j])
        part[:, :, j * 256 : (j + 1) * 256] = res[:64].reshape(8, 8, 256)
        extras = extras + res[64:72]
    for r in range(group8):
        part[r, :, 768:] = extras
    pl.semaphore_wait(barrier, expected)

    def sent(src, dst, ssem, gsem, to):
        return pltpu.make_async_remote_copy(
            src_ref=src, dst_ref=dst, send_sem=ssem, recv_sem=gsem, device_id=to, device_id_type=MESH
        )

    ring1 = []
    for i in range(1, group8):
        q = (me8 + i) % group8
        copy = sent(part.at[q], got1.at[i], s1.at[i], g1.at[i], (wide_of(q, depth), n))
        copy.start()
        ring1.append(copy)

    loads[5].wait()
    for k in range(pairs):
        act_loads[2 * k].wait()
        act_loads[2 * k + 1].wait()
        raw = act_v[2 * k : 2 * k + 2].reshape(256, act.shape[3]).astype(F32)
        acted = (raw / (1.0 + jnp.exp(-raw))).astype(BF16)
        res = dot_t(cw_v[...], acted)
        prod[2 * k] = res[:, :LANES]
        prod[2 * k + 1] = res[:, LANES:]

    full = (16 * (rows + 2), LANES)
    col = lax.broadcasted_iota(jnp.int32, full, 1) % 64
    early = lax.broadcasted_iota(jnp.int32, full, 1) < 64
    taps = []
    for a in range(3):
        moved = []
        for c in range(3):
            planes = []
            for h in range(-1, rows + 1):
                total = None
                for b in range(3):
                    src = h + b - 1
                    if 0 <= src < rows:
                        g = (a * 3 + b) * 3 + c
                        piece = prod[src, 16 * g : 16 * g + 16, :]
                        total = piece if total is None else total + piece
                planes.append(total)
            moved.append(jnp.concatenate(planes, axis=0))
        left = jnp.where(col == 0, 0.0, rolled(moved[0], 1))
        right = jnp.where(col == 63, 0.0, rolled(moved[2], -1))
        taps.append(moved[1] + left + right)
    swapped = rolled(taps[1], 64)
    here = taps[2] + jnp.where(early, 0.0, swapped)
    ahead = taps[0] + jnp.where(early, swapped, 0.0)
    copies = jnp.where(early, taps[1] + taps[0], rolled(taps[0], 64))
    here = here + jnp.where(w == 0, copies, 0.0)
    a_v[...] = here.reshape(rows + 2, 16, LANES)
    b_v[...] = ahead.reshape(rows + 2, 16, LANES)

    up = n > 0
    down = n < narrows - 1
    edges = [
        (b_v.at[pl.ds(1, rows)], bm_v, has_next, has_prev, (w + 1, n)),
        (a_v.at[0], ab_v, up, down, (w, n - 1)),
        (a_v.at[rows + 1], at_v, down, up, (w, n + 1)),
        (b_v.at[0], bb_v, jnp.logical_and(has_next, up), jnp.logical_and(has_prev, down), (w + 1, n - 1)),
        (b_v.at[rows + 1], bt_v, jnp.logical_and(has_next, down), jnp.logical_and(has_prev, up), (w + 1, n + 1)),
    ]
    edge_copies = []
    for k, (src, dst, gives, gets, to) in enumerate(edges):
        copy = sent(src, dst, sh_sem.at[k], gh_sem.at[k], to)
        edge_copies.append(copy)

        @pl.when(gives)
        def _():
            copy.start()

        @pl.when(jnp.logical_not(gets))
        def _():
            dst[...] = jnp.zeros(dst.shape, F32)

    hi, lo = halves(weight - means)
    wst[:64] = hi
    wst[64:] = lo

    for copy in ring1:
        copy.wait_recv()
    total = part[me8]
    for i in range(1, group8):
        total = total + got1[i]
    sum1[...] = total
    ring2 = []
    for i in range(1, DEPTHS):
        z = (depth + i) % DEPTHS
        copy = sent(sum1, got2.at[i], s2.at[i], g2.at[i], (wide_of(me8, z), n))
        copy.start()
        ring2.append(copy)

    for k, (src, dst, gives, gets, to) in enumerate(edges):

        @pl.when(gets)
        def _():
            edge_copies[k].wait_recv()

    lane1 = lax.broadcasted_iota(jnp.int32, (16, LANES), 1)
    pick = jnp.where(
        (lax.broadcasted_iota(jnp.int32, (32, LANES), 1) % 64) // 2
        == lax.broadcasted_iota(jnp.int32, (32, LANES), 0),
        1.0,
        0.0,
    ).astype(BF16)
    latents = []
    for h in range(rows):
        value = a_v[h + 1] + bm_v[h]
        if h == 0:
            value = value + (at_v[...] + bt_v[...])
        if h == rows - 1:
            value = value + (ab_v[...] + bb_v[...])
        latents.append(value)
    patches = []
    for p in range(pairs):
        blocks = []
        for t in range(2):
            for u in range(2):
                for v in range(2):
                    keep = jnp.logical_and(lane1 // 64 == t, lane1 % 2 == v)
                    blocks.append(jnp.where(keep, latents[2 * p + u], 0.0).astype(BF16))
        patches.append(dot_t(pick, jnp.concatenate(blocks, axis=0)))
    x = jnp.concatenate(patches, axis=0)
    x_all[n] = x.astype(BF16)
    ringx = []
    for i in range(1, narrows):
        copy = sent(x_all.at[n], x_all.at[n], sx.at[i], gx.at[i], (w, (n + i) % narrows))
        copy.start()
        ringx.append(copy)

    for copy in ring2:
        copy.wait_recv()
    total = sum1[...]
    for i in range(1, DEPTHS):
        total = total + got2[i]
    m_all[me8] = total[:, :768]
    e_out[...] = total[:, 768:]
    ring3 = []
    for i in range(1, group8):
        q = (me8 + i) % group8
        copy = sent(m_all.at[me8], m_all.at[me8], s3.at[i], g3.at[i], (wide_of(q, depth), n))
        copy.start()
        ring3.append(copy)

    per = x.shape[0]
    other = rolled(x, 64)
    low = lax.broadcasted_iota(jnp.int32, x.shape, 1) < 64
    twice = jnp.concatenate([jnp.where(low, x, other), jnp.where(low, other, x)], axis=0).astype(BF16)
    squares = jnp.zeros((2 * per, LANES), F32)
    step = 512
    for k in range(width // step):
        piece = pl.ds(k * step, step)
        centre = dot(twice, wst[:, piece]) + (pb_v[:, piece] - bias_mean)
        centre = centre * centre
        for i in range(step // LANES):
            squares = squares + centre[:, i * LANES : (i + 1) * LANES]
    spread = jnp.sum(squares, axis=1, keepdims=True) * (1.0 / width)
    factor = lax.rsqrt(spread + 1e-06)
    lane2 = lax.broadcasted_iota(jnp.int32, (per, LANES), 1)
    placed = jnp.where(lane2 == 0, factor[:per], jnp.where(lane2 == 1, factor[per:], 0.0))
    placed = jnp.concatenate([placed, jnp.zeros((LANES - per, LANES), F32)], axis=0)
    r_all[n] = jnp.transpose(placed)[:8]
    ringr = []
    for i in range(1, narrows):
        copy = sent(r_all.at[n], r_all.at[n], sr.at[i], gr.at[i], (w, (n + i) % narrows))
        copy.start()
        ringr.append(copy)

    for copy in ringx:
        copy.wait_recv()
    x_out[...] = x_all[...]
    for copy in ring3:
        copy.wait_recv()
    m_out[...] = m_all[...]
    for copy in ringr:
        copy.wait_recv()
    r_out[...] = r_all[...]
    for copy in ring1 + ring2 + ring3 + ringx + ringr:
        copy.wait_send()
    for k, (src, dst, gives, gets, to) in enumerate(edges):

        @pl.when(gives)
        def _():
            edge_copies[k].wait_send()


def back(x_ref, r_ref, m_ref, e_ref, bias, gains, out, xx, mm, factor, stage, sems):
    tokens = x_ref.shape[0]
    per = tokens // 8
    xx[:, :LANES] = x_ref[...]
    xx[:, LANES:] = x_ref[...]
    hi, lo = halves(m_ref[...])
    mm[...] = jnp.zeros(mm.shape, BF16)
    for t in range(2):
        mm[t, 64 * t : 64 * t + 64] = hi
        mm[t, 128 + 64 * t : 192 + 64 * t] = lo
    flat = r_ref[...]
    turned = jnp.transpose(jnp.concatenate([flat, jnp.zeros((LANES - flat.shape[0], LANES), F32)], axis=0))
    copies = []
    for t in range(2):
        for src in range(8):
            column = turned[:per, 8 * src + t : 8 * src + t + 1]
            factor[t, per * src : per * src + per] = jnp.broadcast_to(column, (per, LANES))
    for t in range(2):
        for j in range(3):
            product = dot(xx[...], mm[t, :, 256 * j : 256 * j + 256])
            rows_b = e_ref[2 * j : 2 * j + 1]
            rows_c = e_ref[2 * j + 1 : 2 * j + 2] + bias[j : j + 1]
            for hd in range(2):
                cols = slice(LANES * hd, LANES * hd + LANES)
                y = (product[:, cols] + rows_b[:, cols]) * factor[t] + rows_c[:, cols]
                if j < 2:
                    mean = jnp.sum(y * y, axis=1, keepdims=True) * (1.0 / LANES)
                    y = y * lax.rsqrt(mean + 1e-06) * gains[j : j + 1]
                stage[3 * t + j, :, cols] = y.astype(BF16)
            copy = pltpu.make_async_copy(
                stage.at[3 * t + j], out.at[j, pl.ds(t * tokens, tokens)], sems.at[3 * t + j]
            )
            copy.start()
            copies.append(copy)
    for copy in copies:
        copy.wait()


def local(wides, narrows, activations, conv_weight, patch_weight, patch_bias, shift, scale, qkv_weight, qkv_bias, norm_gains):
    rows, cols, channels = activations.shape[1:]
    width = patch_weight.shape[1]
    taps = jnp.transpose(conv_weight, (0, 1, 2, 4, 3)).reshape(-1, channels)
    qkv = jnp.transpose(qkv_weight, (1, 0, 2))
    group8 = wides // DEPTHS
    per = rows // 2 * cols // 2
    any_spec = pl.BlockSpec(memory_space=pl.ANY)
    vmem = pl.BlockSpec(memory_space=pltpu.VMEM)
    dma = pltpu.SemaphoreType.DMA
    edge = pltpu.VMEM((16, LANES), F32)
    x, r, m, e = pl.pallas_call(
        functools.partial(front, (wides, narrows, rows, width)),
        out_shape=[
            jax.ShapeDtypeStruct((narrows, per, LANES), BF16),
            jax.ShapeDtypeStruct((narrows, 8, LANES), F32),
            jax.ShapeDtypeStruct((8, 8, 768), F32),
            jax.ShapeDtypeStruct((8, 256), F32),
        ],
        in_specs=[any_spec] * 7,
        out_specs=[vmem] * 4,
        scratch_shapes=[
            pltpu.VMEM((rows, 2, cols, channels), BF16),
            pltpu.VMEM(taps.shape, BF16),
            pltpu.VMEM(patch_weight.shape, BF16),
            pltpu.VMEM((1, width), F32),
            pltpu.VMEM((1, width), F32),
            pltpu.VMEM((1, width), F32),
            pltpu.VMEM((3, LANES, 256), BF16),
            pltpu.VMEM((group8, 8, 1024), F32),
            pltpu.VMEM((group8, 8, 1024), F32),
            pltpu.VMEM((8, 1024), F32),
            pltpu.VMEM((DEPTHS, 8, 1024), F32),
            pltpu.VMEM((8, 1024), F32),
            pltpu.VMEM((8, 8, 768), F32),
            pltpu.VMEM((rows, taps.shape[0], LANES), F32),
            pltpu.VMEM((rows + 2, 16, LANES), F32),
            pltpu.VMEM((rows + 2, 16, LANES), F32),
            edge,
            edge,
            pltpu.VMEM((rows, 16, LANES), F32),
            edge,
            edge,
            pltpu.VMEM((LANES, width), BF16),
            pltpu.VMEM((narrows, per, LANES), BF16),
            pltpu.VMEM((narrows, 8, LANES), F32),
            dma((6,)),
            dma((rows,)),
            dma((group8,)),
            dma((group8,)),
            dma((DEPTHS,)),
            dma((DEPTHS,)),
            dma((group8,)),
            dma((group8,)),
            dma((narrows,)),
            dma((narrows,)),
            dma((narrows,)),
            dma((narrows,)),
            dma((5,)),
            dma((5,)),
        ],
        compiler_params=pltpu.CompilerParams(
            collective_id=0, has_side_effects=True, vmem_limit_bytes=40 * 1024 * 1024
        ),
        name="front",
    )(
        activations,
        taps,
        patch_weight,
        patch_bias.reshape(1, -1),
        shift.reshape(1, -1),
        scale.reshape(1, -1),
        qkv,
    )
    tokens = narrows * per
    return pl.pallas_call(
        back,
        out_shape=jax.ShapeDtypeStruct((3, 2 * tokens, 256), BF16),
        in_specs=[vmem] * 6,
        out_specs=any_spec,
        scratch_shapes=[
            pltpu.VMEM((tokens, 2 * LANES), BF16),
            pltpu.VMEM((2, 256, 768), BF16),
            pltpu.VMEM((2, tokens, LANES), F32),
            pltpu.VMEM((6, tokens, 256), BF16),
            dma((6,)),
        ],
        compiler_params=pltpu.CompilerParams(vmem_limit_bytes=40 * 1024 * 1024),
        name="back",
    )(x.reshape(tokens, LANES), r.reshape(narrows * 8, LANES), m.reshape(64, 768), e, qkv_bias, norm_gains)


def solution(mesh):
    placed = (
        P("wide", "narrow", None, None),
        P(),
        P(),
        P(),
        P(),
        P(),
        P("wide", None, "narrow"),
        P(None, "narrow"),
        P(),
    )
    return jax.shard_map(
        functools.partial(local, mesh.shape["wide"], mesh.shape["narrow"]),
        mesh=mesh,
        in_specs=placed,
        out_specs=P(None, "wide", "narrow"),
        check_vma=False,
    )
```

```python
import functools

import jax
import jax.numpy as jnp
from jax import lax
from jax.experimental import pallas as pl
from jax.experimental.pallas import tpu as pltpu
from jax.sharding import PartitionSpec as P

MESH = pl.DeviceIdType.MESH
F32 = jnp.float32
BF16 = jnp.bfloat16
DEPTHS = 4
CORES = 2
LANES = 128


def rolled(x, by):
    return pltpu.roll(x, by % x.shape[1], 1)


def halves(x):
    high = x.astype(BF16)
    return high, (x - high.astype(F32)).astype(BF16)


def dot(a, b):
    return lax.dot_general(a, b, (((1,), (0,)), ((), ())), preferred_element_type=F32)


def dot_t(a, b):
    return lax.dot_general(a, b, (((1,), (1,)), ((), ())), preferred_element_type=F32)


def front(
    sizes,
    act, cw, pw, pb, sh, sc, qw, qb, ng,
    x_out, m_out, e_out,
    act_v, cw_v, pw_v, pb_v, sh_v, sc_v, qw_v, qb_v, ng_v,
    part, pair, share, got1, own, got2, m_all, prod,
    a_v, b_v, at_v, ab_v, bm_v, bt_v, bb_v,
    wst, x_all, r_all,
    in_sem, act_sem, s0, g0, s1, g1, s3, g3, sx, gx, sh_sem, gh_sem,
):
    wides, narrows, rows, width = sizes
    span = qw.shape[1]
    w = lax.axis_index("wide")
    n = lax.axis_index("narrow")
    pairs = rows // 2
    chips = wides // CORES
    core = w % CORES
    me = w // CORES
    partner = w + 1 - 2 * core
    sums = core == CORES - 1

    chip_y = me // DEPTHS
    chip_z = me % DEPTHS
    highs = chips // DEPTHS
    each = share.shape[1]

    def core1(y, z):
        return (y % highs * DEPTHS + z % DEPTHS) * CORES + CORES - 1, n

    def landed(ref, sem):
        pltpu.make_async_copy(ref, ref, sem).wait()

    loads = []
    for k, (src, dst) in enumerate(
        [(pw, pw_v), (sc, sc_v), (sh, sh_v), (pb, pb_v), (qw, qw_v.at[:, pl.ds(0, span), :]), (cw, cw_v), (qb, qb_v), (ng, ng_v)]
    ):
        copy = pltpu.make_async_copy(src, dst, in_sem.at[k])
        copy.start()
        loads.append(copy)
    for k in range(pairs):
        for t in range(2):
            pltpu.make_async_copy(
                act.at[t, pl.ds(2 * k, 2)], act_v.at[pl.ds(2 * k, 2), t], act_sem.at[k]
            ).start()

    barrier = pltpu.get_barrier_semaphore()

    def greet(wide, narrow):
        pl.semaphore_signal(barrier, inc=1, device_id=(wide, narrow), device_id_type=MESH)

    @pl.when(sums)
    def _():
        for i in range(1, DEPTHS):
            greet(*core1(chip_y, chip_z + i))
        for i in range(1, highs):
            greet(*core1(chip_y + i, chip_z))

    for i in range(1, narrows):
        greet(w, (n + i) % narrows)
    has_next = w < wides - 1
    has_prev = w > 0
    for there, dw in ((has_next, 1), (has_prev, -1)):
        for dn in (-1, 0, 1):
            inside = there
            if dn == -1:
                inside = jnp.logical_and(there, n > 0)
            if dn == 1:
                inside = jnp.logical_and(there, n < narrows - 1)

            @pl.when(inside)
            def _():
                greet(w + dw, n + dn)

    greet(partner, n)
    sides = jnp.where(has_next, 1, 0) + jnp.where(has_prev, 1, 0)
    across = 1 + jnp.where(n > 0, 1, 0) + jnp.where(n < narrows - 1, 1, 0)
    expected = jnp.where(sums, DEPTHS + highs - 1, 1) + (narrows - 1) + sides * across

    qw_v[:, span:, :] = jnp.zeros((3, qw_v.shape[1] - span, qw_v.shape[2]), BF16)
    for copy in loads[:5]:
        copy.wait()
    weight = pw_v[...].astype(F32)
    means = jnp.sum(weight, axis=1, keepdims=True) * (1.0 / width)
    bias_mean = jnp.sum(pb_v[...], axis=1, keepdims=True) * (1.0 / width)
    begin = w * span
    base = pl.multiple_of(jnp.minimum(begin // LANES, width // LANES - 2) * LANES, LANES)
    window = pl.ds(base, 2 * LANES)
    gain = 1.0 + sc_v[:, window]
    main = (pw_v[:, window].astype(F32) - means) * gain
    extra_b = (pb_v[:, window] - bias_mean) * gain
    extra_s = sh_v[:, window]
    pad = jnp.zeros((14, 2 * LANES), F32)
    stacked = jnp.concatenate([main, extra_b, extra_s, pad], axis=0)
    shift_by = (2 * LANES - (begin - base)) % (2 * LANES)
    stacked = pltpu.roll(stacked, shift_by, 1)[:, :LANES]
    lane = lax.broadcasted_iota(jnp.int32, stacked.shape, 1)
    stacked = jnp.where(lane < span, stacked, 0.0)
    hi, lo = halves(stacked)
    for j in range(3):
        res = dot(hi, qw_v[j]) + dot(lo, qw_v[j])
        for head in range(2):
            part[15 * head + 5 * j : 15 * head + 5 * j + 5] = res[:, head * LANES : (head + 1) * LANES].reshape(5, 16, LANES)
    loads[5].wait()
    for k in range(pairs):
        landed(act_v.at[pl.ds(2 * k, 2)], act_sem.at[k])
        raw = act_v[2 * k : 2 * k + 2].reshape(256, act.shape[3]).astype(F32)
        acted = (raw / (1.0 + jnp.exp(-raw))).astype(BF16)
        res = dot_t(cw_v[...], acted)
        prod[2 * k] = res[:, :LANES]
        prod[2 * k + 1] = res[:, LANES:]

    full = (16 * (rows + 2), LANES)
    col = lax.broadcasted_iota(jnp.int32, full, 1) % 64
    early = lax.broadcasted_iota(jnp.int32, full, 1) < 64
    taps = []
    for a in range(3):
        moved = []
        for c in range(3):
            planes = []
            for h in range(-1, rows + 1):
                total = None
                for b in range(3):
                    src = h + b - 1
                    if 0 <= src < rows:
                        g = (a * 3 + b) * 3 + c
                        piece = prod[src, 16 * g : 16 * g + 16, :]
                        total = piece if total is None else total + piece
                planes.append(total)
            moved.append(jnp.concatenate(planes, axis=0))
        left = jnp.where(col == 0, 0.0, rolled(moved[0], 1))
        right = jnp.where(col == 63, 0.0, rolled(moved[2], -1))
        taps.append(moved[1] + left + right)
    swapped = rolled(taps[1], 64)
    here = taps[2] + jnp.where(early, 0.0, swapped)
    ahead = taps[0] + jnp.where(early, swapped, 0.0)
    copies = jnp.where(early, taps[1] + taps[0], rolled(taps[0], 64))
    here = here + jnp.where(w == 0, copies, 0.0)
    a_v[...] = here.reshape(rows + 2, 16, LANES)
    b_v[...] = ahead.reshape(rows + 2, 16, LANES)

    pl.semaphore_wait(barrier, expected)

    def sent(src, dst, ssem, gsem, to):
        return pltpu.make_async_remote_copy(
            src_ref=src, dst_ref=dst, send_sem=ssem, recv_sem=gsem, device_id=to, device_id_type=MESH
        )

    pair_copy = sent(part, pair, s0.at[0], g0.at[0], (partner, n))

    @pl.when(jnp.logical_not(sums))
    def _():
        pair_copy.start()

    up = n > 0
    down = n < narrows - 1
    edges = [
        (b_v.at[pl.ds(1, rows)], bm_v, has_next, has_prev, (w + 1, n)),
        (a_v.at[0], ab_v, up, down, (w, n - 1)),
        (a_v.at[rows + 1], at_v, down, up, (w, n + 1)),
        (b_v.at[0], bb_v, jnp.logical_and(has_next, up), jnp.logical_and(has_prev, down), (w + 1, n - 1)),
        (b_v.at[rows + 1], bt_v, jnp.logical_and(has_next, down), jnp.logical_and(has_prev, up), (w + 1, n + 1)),
    ]
    edge_copies = []
    for k, (src, dst, gives, gets, to) in enumerate(edges):
        copy = sent(src, dst, sh_sem.at[k], gh_sem.at[k], to)
        edge_copies.append(copy)

        @pl.when(gives)
        def _():
            copy.start()

        @pl.when(jnp.logical_not(gets))
        def _():
            dst[...] = jnp.zeros(dst.shape, F32)

    hi, lo = halves(weight - means)
    wst[:64] = hi
    wst[64:] = lo

    row16 = lax.broadcasted_iota(jnp.int32, (16, LANES), 0)
    last = sent(m_all, m_all, s3.at[0], g3.at[0], (partner, n))

    @pl.when(sums)
    def _():
        pair_copy.wait_recv()
        for tile in range(30):
            total = part[tile] + pair[tile]
            if tile % 5 == 4:
                hi = total.astype(BF16).astype(F32)
                total = jnp.where(row16 < 2, hi, pltpu.roll(total - hi, 2, 0))
            share[tile // each, tile % each] = total.astype(BF16)
        for tile in range(30, highs * each):
            share[tile // each, tile % each] = jnp.zeros((16, LANES), BF16)
        for i in range(1, highs):
            sent(
                share.at[(chip_y + i) % highs], got1.at[i - 1], s1.at[0], g1.at[0], core1(chip_y + i, chip_z)
            ).start()

    @pl.when(sums)
    def _():
        landed(got1, g1.at[0])
        total = share[chip_y].astype(F32)
        for i in range(1, highs):
            total = total + got1[i - 1].astype(F32)
        own[...] = total.astype(BF16)
        for i in range(1, DEPTHS):
            sent(own, got2.at[i - 1], s1.at[1], g1.at[1], core1(chip_y, chip_z + i)).start()

    for k, (src, dst, gives, gets, to) in enumerate(edges):

        @pl.when(gets)
        def _():
            edge_copies[k].wait_recv()

    lane1 = lax.broadcasted_iota(jnp.int32, (16, LANES), 1)
    pick = jnp.where(
        (lax.broadcasted_iota(jnp.int32, (32, LANES), 1) % 64) // 2
        == lax.broadcasted_iota(jnp.int32, (32, LANES), 0),
        1.0,
        0.0,
    ).astype(BF16)
    latents = []
    for h in range(rows):
        value = a_v[h + 1] + bm_v[h]
        if h == 0:
            value = value + (at_v[...] + bt_v[...])
        if h == rows - 1:
            value = value + (ab_v[...] + bb_v[...])
        latents.append(value)
    patches = []
    for p in range(pairs):
        blocks = []
        for t in range(2):
            for u in range(2):
                for v in range(2):
                    keep = jnp.logical_and(lane1 // 64 == t, lane1 % 2 == v)
                    blocks.append(jnp.where(keep, latents[2 * p + u], 0.0).astype(BF16))
        patches.append(dot_t(pick, jnp.concatenate(blocks, axis=0)))
    x = jnp.concatenate(patches, axis=0)
    x_all[n] = x.astype(BF16)
    for i in range(1, narrows):
        sent(x_all.at[n], x_all.at[n], sx.at[0], gx.at[0], (w, (n + i) % narrows)).start()

    per = x.shape[0]
    other = rolled(x, 64)
    low = lax.broadcasted_iota(jnp.int32, x.shape, 1) < 64
    twice = jnp.concatenate([jnp.where(low, x, other), jnp.where(low, other, x)], axis=0).astype(BF16)
    squares = jnp.zeros((2 * per, LANES), F32)
    step = 512
    for k in range(width // step):
        piece = pl.ds(k * step, step)
        centre = dot(twice, wst[:, piece]) + (pb_v[:, piece] - bias_mean)
        centre = centre * centre
        for i in range(step // LANES):
            squares = squares + centre[:, i * LANES : (i + 1) * LANES]
    spread = jnp.sum(squares, axis=1, keepdims=True) * (1.0 / width)
    factor = lax.rsqrt(spread + 1e-06)
    lane2 = lax.broadcasted_iota(jnp.int32, (per, LANES), 1)
    placed = jnp.where(lane2 == 0, factor[:per], jnp.where(lane2 == 1, factor[per:], 0.0))
    placed = jnp.concatenate([placed, jnp.zeros((LANES - per, LANES), F32)], axis=0)
    r_all[n] = jnp.transpose(placed)[:8]
    for i in range(1, narrows):
        sent(r_all.at[n], r_all.at[n], sx.at[1], gx.at[1], (w, (n + i) % narrows)).start()

    mine = m_all.at[pl.ds(each * chip_y, each)]

    @pl.when(sums)
    def _():
        landed(got2, g1.at[1])
        total = own[...].astype(F32)
        for i in range(1, DEPTHS):
            total = total + got2[i - 1].astype(F32)
        for k in range(each):
            plain = total[k]
            both = plain + pltpu.roll(plain, 14, 0)
            hi = both.astype(BF16).astype(F32)
            both = jnp.where(row16 < 2, hi, pltpu.roll(both - hi, 2, 0))
            tile = each * chip_y + k
            m_all[tile] = jnp.where(tile % 5 == 4, both, plain).astype(BF16)
        for i in range(1, highs):
            sent(mine, mine, s1.at[2], g1.at[2], core1(chip_y + i, chip_z)).start()

    loads[6].wait()
    loads[7].wait()
    e_out[0:3] = qb_v[...]
    e_out[3:5, :LANES] = ng_v[...]
    landed(x_all.at[pl.ds(0, narrows - 1)], gx.at[0])
    landed(r_all.at[pl.ds(0, narrows - 1)], gx.at[1])
    flat = r_all[...].reshape(narrows * 8, LANES)
    turned = jnp.transpose(jnp.concatenate([flat, jnp.zeros((LANES - narrows * 8, LANES), F32)], axis=0))
    for src in range(narrows):
        theirs = x_all[src].astype(F32)
        for t in range(2):
            column = turned[:per, 8 * src + t : 8 * src + t + 1]
            value = theirs * column
            hi = value.astype(BF16).astype(F32)
            lo = value - hi
            value = jnp.where(low, hi, rolled(lo, 64)) if t == 0 else jnp.where(low, rolled(hi, 64), lo)
            hi = column.astype(BF16).astype(F32)
            more = jnp.where(lane2 == 1, column - hi, jnp.where(lane2 < 3, hi, jnp.where(lane2 < 5, 1.0, 0.0)))
            place = pl.ds((t * narrows + src) * per, per)
            x_out[place, :LANES] = value.astype(BF16)
            x_out[place, LANES:] = more.astype(BF16)
    @pl.when(sums)
    def _():
        landed(m_all.at[pl.ds(0, each * (highs - 1))], g1.at[2])
        last.start()

    @pl.when(jnp.logical_not(sums))
    def _():
        last.wait_recv()

    m_out[...] = m_all[...]
    landed(x_all.at[pl.ds(0, narrows - 1)], sx.at[0])
    landed(r_all.at[pl.ds(0, narrows - 1)], sx.at[1])

    @pl.when(sums)
    def _():
        landed(got1, s1.at[0])
        landed(got2, s1.at[1])
        landed(m_all.at[pl.ds(0, each * (highs - 1))], s1.at[2])
        last.wait_send()

    @pl.when(jnp.logical_not(sums))
    def _():
        pair_copy.wait_send()

    for k, (src, dst, gives, gets, to) in enumerate(edges):

        @pl.when(gives)
        def _():
            edge_copies[k].wait_send()


def back(x_ref, m_ref, e_ref, out, mm, stage, sems):
    tokens = x_ref.shape[0] // 2
    row16 = lax.broadcasted_iota(jnp.int32, (16, LANES), 0)
    mm[144:] = jnp.zeros((112, 768), BF16)
    for head in range(2):
        for j in range(3):
            cols = slice(256 * j + LANES * head, 256 * j + LANES * (head + 1))
            tile = 15 * head + 5 * j
            block = m_ref[tile : tile + 4].reshape(64, LANES)
            mm[:64, cols] = block
            mm[64:128, cols] = block
            extra = m_ref[tile + 4].astype(F32)
            constant = extra[1:2] + extra[3:4] + e_ref[j : j + 1, LANES * head : LANES * (head + 1)]
            high = constant.astype(BF16).astype(F32)
            rows = jnp.where(row16 < 2, extra[0:1], 0.0)
            rows = jnp.where(row16 == 2, extra[2:3], rows)
            rows = jnp.where(row16 == 3, high, rows)
            rows = jnp.where(row16 == 4, constant - high, rows)
            mm[128:144, cols] = rows.astype(BF16)
    copies = []
    for t in range(2):
        for j in range(3):
            product = dot(x_ref[t * tokens : (t + 1) * tokens], mm[:, 256 * j : 256 * j + 256])
            for hd in range(2):
                cols = slice(LANES * hd, LANES * hd + LANES)
                y = product[:, cols]
                if j < 2:
                    mean = jnp.sum(y * y, axis=1, keepdims=True) * (1.0 / LANES)
                    y = y * lax.rsqrt(mean + 1e-06) * e_ref[3 + j : 4 + j, :LANES]
                stage[3 * t + j, :, cols] = y.astype(BF16)
            copy = pltpu.make_async_copy(
                stage.at[3 * t + j], out.at[j, pl.ds(t * tokens, tokens)], sems.at[3 * t + j]
            )
            copy.start()
            copies.append(copy)
    for copy in copies:
        copy.wait()


def local(wides, narrows, activations, conv_weight, patch_weight, patch_bias, shift, scale, qkv_weight, qkv_bias, norm_gains):
    rows, cols, channels = activations.shape[1:]
    width = patch_weight.shape[1]
    taps = jnp.transpose(conv_weight, (0, 1, 2, 4, 3)).reshape(-1, channels)
    qkv = jnp.transpose(qkv_weight, (1, 0, 2))
    highs = wides // (CORES * DEPTHS)
    each = -(-30 // highs)
    per = rows // 2 * cols // 2
    any_spec = pl.BlockSpec(memory_space=pltpu.HBM)
    vmem = pl.BlockSpec(memory_space=pltpu.VMEM)
    dma = pltpu.SemaphoreType.DMA
    edge = pltpu.VMEM((16, LANES), F32)
    x, m, e = pl.pallas_call(
        functools.partial(front, (wides, narrows, rows, width)),
        out_shape=[
            jax.ShapeDtypeStruct((2 * narrows * per, 2 * LANES), BF16),
            jax.ShapeDtypeStruct((highs * each, 16, LANES), BF16),
            jax.ShapeDtypeStruct((8, 256), F32),
        ],
        in_specs=[any_spec] * 9,
        out_specs=[vmem] * 3,
        scratch_shapes=[
            pltpu.VMEM((rows, 2, cols, channels), BF16),
            pltpu.VMEM(taps.shape, BF16),
            pltpu.VMEM(patch_weight.shape, BF16),
            pltpu.VMEM((1, width), F32),
            pltpu.VMEM((1, width), F32),
            pltpu.VMEM((1, width), F32),
            pltpu.VMEM((3, LANES, 256), BF16),
            pltpu.VMEM(qkv_bias.shape, F32),
            pltpu.VMEM(norm_gains.shape, F32),
            pltpu.VMEM((30, 16, LANES), F32),
            pltpu.VMEM((30, 16, LANES), F32),
            pltpu.VMEM((highs, each, 16, LANES), BF16),
            pltpu.VMEM((highs - 1, each, 16, LANES), BF16),
            pltpu.VMEM((each, 16, LANES), BF16),
            pltpu.VMEM((DEPTHS - 1, each, 16, LANES), BF16),
            pltpu.VMEM((highs * each, 16, LANES), BF16),
            pltpu.VMEM((rows, taps.shape[0], LANES), F32),
            pltpu.VMEM((rows + 2, 16, LANES), F32),
            pltpu.VMEM((rows + 2, 16, LANES), F32),
            edge,
            edge,
            pltpu.VMEM((rows, 16, LANES), F32),
            edge,
            edge,
            pltpu.VMEM((LANES, width), BF16),
            pltpu.VMEM((narrows, per, LANES), BF16),
            pltpu.VMEM((narrows, 8, LANES), F32),
            dma((8,)),
            dma((rows // 2,)),
            dma((1,)),
            dma((1,)),
            dma((3,)),
            dma((3,)),
            dma((1,)),
            dma((1,)),
            dma((2,)),
            dma((2,)),
            dma((5,)),
            dma((5,)),
        ],
        compiler_params=pltpu.CompilerParams(
            collective_id=0, has_side_effects=True, vmem_limit_bytes=40 * 1024 * 1024
        ),
        name="front",
    )(
        *(
            pltpu.with_memory_space_constraint(a, pltpu.HBM)
            for a in (
                activations,
                taps,
                patch_weight,
                patch_bias.reshape(1, -1),
                shift.reshape(1, -1),
                scale.reshape(1, -1),
                qkv,
                qkv_bias,
                norm_gains,
            )
        )
    )
    tokens = narrows * per
    return pl.pallas_call(
        back,
        out_shape=jax.ShapeDtypeStruct((3, 2 * tokens, 256), BF16),
        in_specs=[vmem] * 3,
        out_specs=any_spec,
        scratch_shapes=[
            pltpu.VMEM((2 * LANES, 768), BF16),
            pltpu.VMEM((6, tokens, 256), BF16),
            dma((6,)),
        ],
        compiler_params=pltpu.CompilerParams(vmem_limit_bytes=40 * 1024 * 1024),
        name="back",
    )(x, m, e)


def solution(mesh):
    placed = (
        P("wide", "narrow", None, None),
        P(),
        P(),
        P(),
        P(),
        P(),
        P("wide", None, "narrow"),
        P(None, "narrow"),
        P(),
    )
    return jax.shard_map(
        functools.partial(local, mesh.shape["wide"], mesh.shape["narrow"]),
        mesh=mesh,
        in_specs=placed,
        out_specs=P(None, "wide", "narrow"),
        check_vma=False,
    )
```

```python
import functools

import jax
import jax.numpy as jnp
from jax import lax
from jax.experimental import pallas as pl
from jax.experimental.pallas import tpu as pltpu
from jax.sharding import PartitionSpec as P

MESH = pl.DeviceIdType.MESH
F32 = jnp.float32
BF16 = jnp.bfloat16
DEPTHS = 4
CORES = 2
LANES = 128


def rolled(x, by):
    return pltpu.roll(x, by % x.shape[1], 1)


def halves(x):
    high = x.astype(BF16)
    return high, (x - high.astype(F32)).astype(BF16)


def dot(a, b):
    return lax.dot_general(a, b, (((1,), (0,)), ((), ())), preferred_element_type=F32)


def dot_t(a, b):
    return lax.dot_general(a, b, (((1,), (1,)), ((), ())), preferred_element_type=F32)


def front(
    sizes,
    act, cw, pw, pb, sh, sc, qw, qb, ng,
    x_out, m_out, e_out,
    act_v, cw_v, pw_v, pb_v, sh_v, sc_v, qw_v, qb_v, ng_v,
    part, pair, share, got1, own, own32, got2, m_all, prod,
    a_v, b_v, at_v, ab_v, bm_v, bt_v, bb_v,
    wst, x_all, r_all,
    in_sem, act_sem, go, s0, g0, s1, g1, sx, gx, sh_sem, gh_sem,
):
    wides, narrows, rows, width = sizes
    span = qw.shape[1]
    w = lax.axis_index("wide")
    n = lax.axis_index("narrow")
    pairs = rows // 2
    chips = wides // CORES
    core = w % CORES
    me = w // CORES
    partner = w + 1 - 2 * core
    sums = core == CORES - 1

    chip_y = me // DEPTHS
    chip_z = me % DEPTHS
    highs = chips // DEPTHS
    half = share.shape[2]
    each = 2 * half

    def at(y, z, c):
        return (y % highs * DEPTHS + z % DEPTHS) * CORES + c, n

    def core1(y, z):
        return at(y, z, CORES - 1)

    def landed(ref, sem):
        pltpu.make_async_copy(ref, ref, sem).wait()

    loads = []
    for k, (src, dst) in enumerate(
        [(pw, pw_v), (sc, sc_v), (sh, sh_v), (pb, pb_v), (qw, qw_v.at[:, pl.ds(0, span), :]), (cw, cw_v), (qb, qb_v), (ng, ng_v)]
    ):
        copy = pltpu.make_async_copy(src, dst, in_sem.at[k])
        copy.start()
        loads.append(copy)
    for k in range(pairs):
        for t in range(2):
            pltpu.make_async_copy(
                act.at[t, pl.ds(2 * k, 2)], act_v.at[pl.ds(2 * k, 2), t], act_sem.at[k]
            ).start()

    barrier = pltpu.get_barrier_semaphore()

    def greet(wide, narrow):
        pl.semaphore_signal(barrier, inc=1, device_id=(wide, narrow), device_id_type=MESH)

    has_next = w < wides - 1
    has_prev = w > 0
    up = n > 0
    down = n < narrows - 1
    for i in range(1, highs):
        greet(*core1(chip_y + i, chip_z))
    for i in range(1, narrows):
        greet(w + CORES - 1 - core, (n + i) % narrows)
    greet(partner, n)

    @pl.when(sums)
    def _():
        for i in range(1, DEPTHS):
            greet(*core1(chip_y, chip_z + i))

        @pl.when(up)
        def _():
            greet(w, n - 1)

        @pl.when(down)
        def _():
            greet(w, n + 1)

    @pl.when(jnp.logical_and(jnp.logical_not(sums), has_prev))
    def _():
        greet(w - 1, n)

        @pl.when(up)
        def _():
            greet(w - 1, n - 1)

        @pl.when(down)
        def _():
            greet(w - 1, n + 1)

    across = jnp.where(up, 1, 0) + jnp.where(down, 1, 0)
    expected = CORES * (narrows - 1) + across + jnp.where(has_next, 1 + across, 0) + CORES * (highs - 1) + DEPTHS

    qw_v[:, span:, :] = jnp.zeros((3, qw_v.shape[1] - span, qw_v.shape[2]), BF16)
    for copy in loads[:5]:
        copy.wait()
    weight = pw_v[...].astype(F32)
    means = jnp.sum(weight, axis=1, keepdims=True) * (1.0 / width)
    bias_mean = jnp.sum(pb_v[...], axis=1, keepdims=True) * (1.0 / width)
    begin = w * span
    base = pl.multiple_of(jnp.minimum(begin // LANES, width // LANES - 2) * LANES, LANES)
    window = pl.ds(base, 2 * LANES)
    gain = 1.0 + sc_v[:, window]
    main = (pw_v[:, window].astype(F32) - means) * gain
    extra_b = (pb_v[:, window] - bias_mean) * gain
    extra_s = sh_v[:, window]
    pad = jnp.zeros((14, 2 * LANES), F32)
    stacked = jnp.concatenate([main, extra_b, extra_s, pad], axis=0)
    shift_by = (2 * LANES - (begin - base)) % (2 * LANES)
    stacked = pltpu.roll(stacked, shift_by, 1)[:, :LANES]
    lane = lax.broadcasted_iota(jnp.int32, stacked.shape, 1)
    stacked = jnp.where(lane < span, stacked, 0.0)
    hi, lo = halves(stacked)
    for j in range(3):
        res = dot(hi, qw_v[j]) + dot(lo, qw_v[j])
        for head in range(2):
            part[15 * head + 5 * j : 15 * head + 5 * j + 5] = res[:, head * LANES : (head + 1) * LANES].reshape(5, 16, LANES)
    def sent(src, dst, ssem, gsem, to):
        return pltpu.make_async_remote_copy(
            src_ref=src, dst_ref=dst, send_sem=ssem, recv_sem=gsem, device_id=to, device_id_type=MESH
        )

    pair_copy = sent(part, pair, s0.at[0], g0.at[0], (partner, n))

    @pl.when(jnp.logical_not(sums))
    def _():
        pl.semaphore_wait(barrier, 1)
        pair_copy.start()

    loads[5].wait()
    for k in range(pairs):
        landed(act_v.at[pl.ds(2 * k, 2)], act_sem.at[k])
    for k in range(pairs):
        raw = act_v[2 * k : 2 * k + 2].reshape(256, act.shape[3]).astype(F32)
        less = 0.5 * raw
        acted = (less + less * jnp.tanh(less)).astype(BF16)
        res = dot_t(cw_v[...], acted)
        prod[2 * k] = res[:, :LANES]
        prod[2 * k + 1] = res[:, LANES:]

    full = (16 * (rows + 2), LANES)
    col = lax.broadcasted_iota(jnp.int32, full, 1) % 64
    early = lax.broadcasted_iota(jnp.int32, full, 1) < 64
    taps = []
    for a in range(3):
        moved = []
        for c in range(3):
            planes = []
            for h in range(-1, rows + 1):
                total = None
                for b in range(3):
                    src = h + b - 1
                    if 0 <= src < rows:
                        g = (a * 3 + b) * 3 + c
                        piece = prod[src, 16 * g : 16 * g + 16, :]
                        total = piece if total is None else total + piece
                planes.append(total)
            moved.append(jnp.concatenate(planes, axis=0))
        left = jnp.where(col == 0, 0.0, rolled(moved[0], 1))
        right = jnp.where(col == 63, 0.0, rolled(moved[2], -1))
        taps.append(moved[1] + left + right)
    swapped = rolled(taps[1], 64)
    here = taps[2] + jnp.where(early, 0.0, swapped)
    ahead = taps[0] + jnp.where(early, swapped, 0.0)
    copies = jnp.where(early, taps[1] + taps[0], rolled(taps[0], 64))
    here = here + jnp.where(w == 0, copies, 0.0)
    a_v[...] = here.reshape(rows + 2, 16, LANES)
    b_v[...] = ahead.reshape(rows + 2, 16, LANES)


    @pl.when(sums)
    def _():
        pl.semaphore_wait(barrier, expected)
        pl.semaphore_signal(go, inc=1, device_id=(partner, n), device_id_type=MESH)

    @pl.when(jnp.logical_not(sums))
    def _():
        pl.semaphore_wait(go, 1)

    edges = [
        (b_v.at[pl.ds(1, rows)], bm_v, has_next, has_prev, (w + 1, n)),
        (a_v.at[0], ab_v, up, down, (w, n - 1)),
        (a_v.at[rows + 1], at_v, down, up, (w, n + 1)),
        (b_v.at[0], bb_v, jnp.logical_and(has_next, up), jnp.logical_and(has_prev, down), (w + 1, n - 1)),
        (b_v.at[rows + 1], bt_v, jnp.logical_and(has_next, down), jnp.logical_and(has_prev, up), (w + 1, n + 1)),
    ]
    edge_copies = []
    for k, (src, dst, gives, gets, to) in enumerate(edges):
        copy = sent(src, dst, sh_sem.at[k], gh_sem.at[k], to)
        edge_copies.append(copy)

        @pl.when(gives)
        def _():
            copy.start()

        @pl.when(jnp.logical_not(gets))
        def _():
            dst[...] = jnp.zeros(dst.shape, F32)

    hi, lo = halves(weight - means)
    wst[:64] = hi
    wst[64:] = lo

    row16 = lax.broadcasted_iota(jnp.int32, (16, LANES), 0)

    @pl.when(sums)
    def _():
        pair_copy.wait_recv()
        for tile in range(30):
            total = part[tile] + pair[tile]
            if tile % 5 == 4:
                hi = total.astype(BF16).astype(F32)
                total = jnp.where(row16 < 2, hi, pltpu.roll(total - hi, 2, 0))
            share[tile % each // half, tile // each, tile % half] = total.astype(BF16)
        for tile in range(30, highs * each):
            share[tile % each // half, tile // each, tile % half] = jnp.zeros((16, LANES), BF16)
        for p in range(2):
            for i in range(1, highs):
                to = (chip_y + i) % highs
                sent(share.at[p, to], got1.at[p, i - 1], s1.at[p], g1.at[p], core1(to, chip_z)).start()

    @pl.when(sums)
    def _():
        for p in range(2):
            landed(got1.at[p], g1.at[p])
            total = share[p, chip_y].astype(F32)
            for i in range(1, highs):
                total = total + got1[p, i - 1].astype(F32)
            own32[p] = total
            own[p] = total.astype(BF16)
            for i in range(1, DEPTHS):
                sent(own.at[p], got2.at[p, i - 1], s1.at[2 + p], g1.at[2 + p], core1(chip_y, chip_z + i)).start()

    for k, (src, dst, gives, gets, to) in enumerate(edges):

        @pl.when(gets)
        def _():
            edge_copies[k].wait_recv()

    lane1 = lax.broadcasted_iota(jnp.int32, (16, LANES), 1)
    pick = jnp.where(
        (lax.broadcasted_iota(jnp.int32, (32, LANES), 1) % 64) // 2
        == lax.broadcasted_iota(jnp.int32, (32, LANES), 0),
        1.0,
        0.0,
    ).astype(BF16)
    latents = []
    for h in range(rows):
        value = a_v[h + 1] + bm_v[h]
        if h == 0:
            value = value + (at_v[...] + bt_v[...])
        if h == rows - 1:
            value = value + (ab_v[...] + bb_v[...])
        latents.append(value)
    patches = []
    for p in range(pairs):
        blocks = []
        for t in range(2):
            for u in range(2):
                for v in range(2):
                    keep = jnp.logical_and(lane1 // 64 == t, lane1 % 2 == v)
                    blocks.append(jnp.where(keep, latents[2 * p + u], 0.0).astype(BF16))
        patches.append(dot_t(pick, jnp.concatenate(blocks, axis=0)))
    x = jnp.concatenate(patches, axis=0)
    x_all[n] = x.astype(BF16)
    for i in range(1, narrows):
        sent(x_all.at[n], x_all.at[n], sx.at[0], gx.at[0], (w, (n + i) % narrows)).start()

    per = x.shape[0]
    other = rolled(x, 64)
    low = lax.broadcasted_iota(jnp.int32, x.shape, 1) < 64
    twice = jnp.concatenate([jnp.where(low, x, other), jnp.where(low, other, x)], axis=0).astype(BF16)
    squares = jnp.zeros((2 * per, LANES), F32)
    step = 512
    for k in range(width // step):
        piece = pl.ds(k * step, step)
        centre = dot(twice, wst[:, piece]) + (pb_v[:, piece] - bias_mean)
        centre = centre * centre
        for i in range(step // LANES):
            squares = squares + centre[:, i * LANES : (i + 1) * LANES]
    spread = jnp.sum(squares, axis=1, keepdims=True) * (1.0 / width)
    factor = lax.rsqrt(spread + 1e-06)
    lane2 = lax.broadcasted_iota(jnp.int32, (per, LANES), 1)
    placed = jnp.where(lane2 == 0, factor[:per], jnp.where(lane2 == 1, factor[per:], 0.0))
    placed = jnp.concatenate([placed, jnp.zeros((LANES - per, LANES), F32)], axis=0)
    r_all[n] = jnp.transpose(placed)[:8]
    for i in range(1, narrows):
        sent(r_all.at[n], r_all.at[n], sx.at[1], gx.at[1], (w, (n + i) % narrows)).start()

    @pl.when(sums)
    def _():
        for p in range(2):
            landed(got2.at[p], g1.at[2 + p])
            total = own32[p]
            for i in range(1, DEPTHS):
                total = total + got2[p, i - 1].astype(F32)
            for k in range(half):
                plain = total[k]
                both = plain + pltpu.roll(plain, 14, 0)
                hi = both.astype(BF16).astype(F32)
                both = jnp.where(row16 < 2, hi, pltpu.roll(both - hi, 2, 0))
                tile = each * chip_y + half * p + k
                m_all[tile] = jnp.where(tile % 5 == 4, both, plain).astype(BF16)
            mine = m_all.at[pl.ds(each * chip_y + half * p, half)]
            for i in range(highs):
                for c in range(CORES):
                    if i > 0 or c < CORES - 1:
                        sent(mine, mine, s1.at[4], g1.at[4], at(chip_y + i, chip_z, c)).start()

    loads[6].wait()
    loads[7].wait()
    e_out[0:3] = qb_v[...]
    e_out[3:5, :LANES] = ng_v[...]
    landed(x_all.at[pl.ds(0, narrows - 1)], gx.at[0])
    landed(r_all.at[pl.ds(0, narrows - 1)], gx.at[1])
    flat = r_all[...].reshape(narrows * 8, LANES)
    turned = jnp.transpose(jnp.concatenate([flat, jnp.zeros((LANES - narrows * 8, LANES), F32)], axis=0))
    for src in range(narrows):
        theirs = x_all[src].astype(F32)
        columns = [
            jnp.broadcast_to(turned[:per, 8 * src + t : 8 * src + t + 1], (per, LANES)) for t in range(2)
        ]
        value = theirs * jnp.where(low, columns[0], columns[1])
        hi = value.astype(BF16).astype(F32)
        lo = value - hi
        values = [jnp.where(low, hi, rolled(lo, 64)), jnp.where(low, rolled(hi, 64), lo)]
        for t in range(2):
            hi = columns[t].astype(BF16).astype(F32)
            more = jnp.where(lane2 == 1, columns[t] - hi, jnp.where(lane2 < 3, hi, 1.0))
            place = pl.ds((t * narrows + src) * per, per)
            x_out[place, :LANES] = values[t].astype(BF16)
            x_out[place, LANES:] = more.astype(BF16)
    @pl.when(sums)
    def _():
        landed(m_all.at[pl.ds(0, each * (highs - 1))], g1.at[4])

    @pl.when(jnp.logical_not(sums))
    def _():
        landed(m_all, g1.at[4])

    m_out[...] = m_all[...]
    landed(x_all.at[pl.ds(0, narrows - 1)], sx.at[0])
    landed(r_all.at[pl.ds(0, narrows - 1)], sx.at[1])

    @pl.when(sums)
    def _():
        for p in range(2):
            landed(got1.at[p], s1.at[p])
            landed(got2.at[p], s1.at[2 + p])
        landed(m_all, s1.at[4])
        landed(m_all.at[pl.ds(0, each * (highs - 1))], s1.at[4])

    @pl.when(jnp.logical_not(sums))
    def _():
        pair_copy.wait_send()

    for k, (src, dst, gives, gets, to) in enumerate(edges):

        @pl.when(gives)
        def _():
            edge_copies[k].wait_send()


def back(x_ref, m_ref, e_ref, out, mm, stage, sems):
    tokens = x_ref.shape[0] // 2
    row16 = lax.broadcasted_iota(jnp.int32, (16, LANES), 0)
    mm[144:] = jnp.zeros((112, 768), BF16)
    for head in range(2):
        for j in range(3):
            cols = slice(256 * j + LANES * head, 256 * j + LANES * (head + 1))
            tile = 15 * head + 5 * j
            block = m_ref[tile : tile + 4].reshape(64, LANES)
            mm[:64, cols] = block
            mm[64:128, cols] = block
            extra = m_ref[tile + 4].astype(F32)
            constant = extra[1:2] + extra[3:4] + e_ref[j : j + 1, LANES * head : LANES * (head + 1)]
            high = constant.astype(BF16).astype(F32)
            rows = jnp.where(row16 < 2, extra[0:1], 0.0)
            rows = jnp.where(row16 == 2, extra[2:3], rows)
            rows = jnp.where(row16 == 3, high, rows)
            rows = jnp.where(row16 == 4, constant - high, rows)
            mm[128:144, cols] = rows.astype(BF16)
    copies = []
    half = tokens // 2
    for part in range(4):
        for j in range(3):
            place = pl.ds(part * half, half)
            product = dot(x_ref[place], mm[:, 256 * j : 256 * j + 256])
            for hd in range(2):
                cols = slice(LANES * hd, LANES * hd + LANES)
                y = product[:, cols]
                if j < 2:
                    mean = jnp.sum(y * y, axis=1, keepdims=True) * (1.0 / LANES)
                    y = y * lax.rsqrt(mean + 1e-06) * e_ref[3 + j : 4 + j, :LANES]
                stage[j, place, cols] = y.astype(BF16)
            copy = pltpu.make_async_copy(stage.at[j, place], out.at[j, place], sems.at[3 * part + j])
            copy.start()
            copies.append(copy)
    for copy in copies:
        copy.wait()


def local(wides, narrows, activations, conv_weight, patch_weight, patch_bias, shift, scale, qkv_weight, qkv_bias, norm_gains):
    rows, cols, channels = activations.shape[1:]
    width = patch_weight.shape[1]
    taps = jnp.transpose(conv_weight, (0, 1, 2, 4, 3)).reshape(-1, channels)
    qkv = jnp.transpose(qkv_weight, (1, 0, 2))
    highs = wides // (CORES * DEPTHS)
    half = -(-30 // (2 * highs))
    per = rows // 2 * cols // 2
    any_spec = pl.BlockSpec(memory_space=pltpu.HBM)
    vmem = pl.BlockSpec(memory_space=pltpu.VMEM)
    dma = pltpu.SemaphoreType.DMA
    edge = pltpu.VMEM((16, LANES), F32)
    x, m, e = pl.pallas_call(
        functools.partial(front, (wides, narrows, rows, width)),
        out_shape=[
            jax.ShapeDtypeStruct((2 * narrows * per, 2 * LANES), BF16),
            jax.ShapeDtypeStruct((highs * 2 * half, 16, LANES), BF16),
            jax.ShapeDtypeStruct((8, 256), F32),
        ],
        in_specs=[any_spec] * 9,
        out_specs=[vmem] * 3,
        scratch_shapes=[
            pltpu.VMEM((rows, 2, cols, channels), BF16),
            pltpu.VMEM(taps.shape, BF16),
            pltpu.VMEM(patch_weight.shape, BF16),
            pltpu.VMEM((1, width), F32),
            pltpu.VMEM((1, width), F32),
            pltpu.VMEM((1, width), F32),
            pltpu.VMEM((3, LANES, 256), BF16),
            pltpu.VMEM(qkv_bias.shape, F32),
            pltpu.VMEM(norm_gains.shape, F32),
            pltpu.VMEM((30, 16, LANES), F32),
            pltpu.VMEM((30, 16, LANES), F32),
            pltpu.VMEM((2, highs, half, 16, LANES), BF16),
            pltpu.VMEM((2, highs - 1, half, 16, LANES), BF16),
            pltpu.VMEM((2, half, 16, LANES), BF16),
            pltpu.VMEM((2, half, 16, LANES), F32),
            pltpu.VMEM((2, DEPTHS - 1, half, 16, LANES), BF16),
            pltpu.VMEM((highs * 2 * half, 16, LANES), BF16),
            pltpu.VMEM((rows, taps.shape[0], LANES), F32),
            pltpu.VMEM((rows + 2, 16, LANES), F32),
            pltpu.VMEM((rows + 2, 16, LANES), F32),
            edge,
            edge,
            pltpu.VMEM((rows, 16, LANES), F32),
            edge,
            edge,
            pltpu.VMEM((LANES, width), BF16),
            pltpu.VMEM((narrows, per, LANES), BF16),
            pltpu.VMEM((narrows, 8, LANES), F32),
            dma((8,)),
            dma((rows // 2,)),
            pltpu.SemaphoreType.REGULAR,
            dma((1,)),
            dma((1,)),
            dma((5,)),
            dma((5,)),
            dma((2,)),
            dma((2,)),
            dma((5,)),
            dma((5,)),
        ],
        compiler_params=pltpu.CompilerParams(
            collective_id=0, has_side_effects=True, vmem_limit_bytes=40 * 1024 * 1024
        ),
        name="front",
    )(
        *(
            pltpu.with_memory_space_constraint(a, pltpu.HBM)
            for a in (
                activations,
                taps,
                patch_weight,
                patch_bias.reshape(1, -1),
                shift.reshape(1, -1),
                scale.reshape(1, -1),
                qkv,
                qkv_bias,
                norm_gains,
            )
        )
    )
    tokens = narrows * per
    return pl.pallas_call(
        back,
        out_shape=jax.ShapeDtypeStruct((3, 2 * tokens, 256), BF16),
        in_specs=[vmem] * 3,
        out_specs=any_spec,
        scratch_shapes=[
            pltpu.VMEM((2 * LANES, 768), BF16),
            pltpu.VMEM((3, 2 * tokens, 256), BF16),
            dma((12,)),
        ],
        compiler_params=pltpu.CompilerParams(vmem_limit_bytes=40 * 1024 * 1024),
        name="back",
    )(x, m, e)


def solution(mesh):
    placed = (
        P("wide", "narrow", None, None),
        P(),
        P(),
        P(),
        P(),
        P(),
        P("wide", None, "narrow"),
        P(None, "narrow"),
        P(),
    )
    return jax.shard_map(
        functools.partial(local, mesh.shape["wide"], mesh.shape["narrow"]),
        mesh=mesh,
        in_specs=placed,
        out_specs=P(None, "wide", "narrow"),
        check_vma=False,
    )
```

```python
import functools

import jax
import jax.numpy as jnp
from jax import lax
from jax.experimental import pallas as pl
from jax.experimental.pallas import tpu as pltpu
from jax.sharding import PartitionSpec as P

MESH = pl.DeviceIdType.MESH
F32 = jnp.float32
BF16 = jnp.bfloat16
DEPTHS = 4
CORES = 2
LANES = 128


def rolled(x, by):
    return pltpu.roll(x, by % x.shape[1], 1)


def halves(x):
    high = x.astype(BF16)
    return high, (x - high.astype(F32)).astype(BF16)


def dot(a, b):
    return lax.dot_general(a, b, (((1,), (0,)), ((), ())), preferred_element_type=F32)


def dot_t(a, b):
    return lax.dot_general(a, b, (((1,), (1,)), ((), ())), preferred_element_type=F32)


def front(
    sizes,
    act, cw, pw, pb, sh, sc, qw, qb, ng,
    x_out, m_out, e_out,
    act_v, cw_v, pw_v, pb_v, sh_v, sc_v, qw_v, qb_v, ng_v,
    part, pair, share, got1, own, own32, got2, m_all, prod,
    a_v, b_v, at_v, ab_v, bm_v, bt_v, bb_v,
    wst, x_all, r_all,
    in_sem, act_sem, go, s0, g0, s1, g1, sx, gx, sh_sem, gh_sem,
):
    wides, narrows, rows, width = sizes
    span = qw.shape[1]
    w = lax.axis_index("wide")
    n = lax.axis_index("narrow")
    pairs = rows // 2
    chips = wides // CORES
    core = w % CORES
    me = w // CORES
    partner = w + 1 - 2 * core
    sums = core == CORES - 1

    chip_y = me // DEPTHS
    chip_z = me % DEPTHS
    highs = chips // DEPTHS
    half = share.shape[2]
    each = 2 * half

    def at(y, z, c):
        return (y % highs * DEPTHS + z % DEPTHS) * CORES + c, n

    def core1(y, z):
        return at(y, z, CORES - 1)

    def landed(ref, sem):
        pltpu.make_async_copy(ref, ref, sem).wait()

    loads = []
    for k, (src, dst) in enumerate(
        [(pw, pw_v), (sc, sc_v), (sh, sh_v), (pb, pb_v), (qw, qw_v.at[:, pl.ds(0, span), :]), (cw, cw_v), (qb, qb_v), (ng, ng_v)]
    ):
        copy = pltpu.make_async_copy(src, dst, in_sem.at[k])
        copy.start()
        loads.append(copy)
    for k in range(pairs):
        for t in range(2):
            pltpu.make_async_copy(
                act.at[t, pl.ds(2 * k, 2)], act_v.at[pl.ds(2 * k, 2), t], act_sem.at[k]
            ).start()

    barrier = pltpu.get_barrier_semaphore()

    def greet(wide, narrow):
        pl.semaphore_signal(barrier, inc=1, device_id=(wide, narrow), device_id_type=MESH)

    has_next = w < wides - 1
    has_prev = w > 0
    up = n > 0
    down = n < narrows - 1
    for i in range(1, highs):
        greet(*core1(chip_y + i, chip_z))
    for other in range(narrows):

        @pl.when(jnp.logical_or(n < other, n == other + 1))
        def _():
            greet(w + CORES - 1 - core, other)

    greet(partner, n)

    @pl.when(sums)
    def _():
        for i in range(1, DEPTHS):
            greet(*core1(chip_y, chip_z + i))

        @pl.when(up)
        def _():
            greet(w, n - 1)

        @pl.when(down)
        def _():
            greet(w, n + 1)

    @pl.when(jnp.logical_and(jnp.logical_not(sums), has_prev))
    def _():
        greet(w - 1, n)

        @pl.when(up)
        def _():
            greet(w - 1, n - 1)

        @pl.when(down)
        def _():
            greet(w - 1, n + 1)

    across = jnp.where(up, 1, 0) + jnp.where(down, 1, 0)
    expected = CORES * (n + jnp.where(down, 1, 0)) + across + jnp.where(has_next, 1 + across, 0) + CORES * (highs - 1) + DEPTHS

    qw_v[:, span:, :] = jnp.zeros((3, qw_v.shape[1] - span, qw_v.shape[2]), BF16)
    for copy in loads[:5]:
        copy.wait()
    weight = pw_v[...].astype(F32)
    means = jnp.sum(weight, axis=1, keepdims=True) * (1.0 / width)
    bias_mean = jnp.sum(pb_v[...], axis=1, keepdims=True) * (1.0 / width)
    begin = w * span
    base = pl.multiple_of(jnp.minimum(begin // LANES, width // LANES - 2) * LANES, LANES)
    window = pl.ds(base, 2 * LANES)
    gain = 1.0 + sc_v[:, window]
    main = (pw_v[:, window].astype(F32) - means) * gain
    extra_b = (pb_v[:, window] - bias_mean) * gain
    extra_s = sh_v[:, window]
    pad = jnp.zeros((14, 2 * LANES), F32)
    stacked = jnp.concatenate([main, extra_b, extra_s, pad], axis=0)
    shift_by = (2 * LANES - (begin - base)) % (2 * LANES)
    stacked = pltpu.roll(stacked, shift_by, 1)[:, :LANES]
    lane = lax.broadcasted_iota(jnp.int32, stacked.shape, 1)
    stacked = jnp.where(lane < span, stacked, 0.0)
    hi, lo = halves(stacked)
    for j in range(3):
        res = dot(hi, qw_v[j]) + dot(lo, qw_v[j])
        for head in range(2):
            part[15 * head + 5 * j : 15 * head + 5 * j + 5] = res[:, head * LANES : (head + 1) * LANES].reshape(5, 16, LANES)
    def sent(src, dst, ssem, gsem, to):
        return pltpu.make_async_remote_copy(
            src_ref=src, dst_ref=dst, send_sem=ssem, recv_sem=gsem, device_id=to, device_id_type=MESH
        )

    pair_copy = sent(part, pair, s0.at[0], g0.at[0], (partner, n))

    @pl.when(jnp.logical_not(sums))
    def _():
        pl.semaphore_wait(barrier, 1)
        pair_copy.start()

    loads[5].wait()
    for k in range(pairs):
        landed(act_v.at[pl.ds(2 * k, 2)], act_sem.at[k])
    for k in range(pairs):
        raw = act_v[2 * k : 2 * k + 2].reshape(256, act.shape[3]).astype(F32)
        less = 0.5 * raw
        acted = (less + less * jnp.tanh(less)).astype(BF16)
        res = dot_t(cw_v[...], acted)
        prod[2 * k] = res[:, :LANES]
        prod[2 * k + 1] = res[:, LANES:]

    full = (16 * (rows + 2), LANES)
    col = lax.broadcasted_iota(jnp.int32, full, 1) % 64
    early = lax.broadcasted_iota(jnp.int32, full, 1) < 64
    taps = []
    for a in range(3):
        moved = []
        for c in range(3):
            planes = []
            for h in range(-1, rows + 1):
                total = None
                for b in range(3):
                    src = h + b - 1
                    if 0 <= src < rows:
                        g = (a * 3 + b) * 3 + c
                        piece = prod[src, 16 * g : 16 * g + 16, :]
                        total = piece if total is None else total + piece
                planes.append(total)
            moved.append(jnp.concatenate(planes, axis=0))
        left = jnp.where(col == 0, 0.0, rolled(moved[0], 1))
        right = jnp.where(col == 63, 0.0, rolled(moved[2], -1))
        taps.append(moved[1] + left + right)
    swapped = rolled(taps[1], 64)
    here = taps[2] + jnp.where(early, 0.0, swapped)
    ahead = taps[0] + jnp.where(early, swapped, 0.0)
    copies = jnp.where(early, taps[1] + taps[0], rolled(taps[0], 64))
    here = here + jnp.where(w == 0, copies, 0.0)
    a_v[...] = here.reshape(rows + 2, 16, LANES)
    b_v[...] = ahead.reshape(rows + 2, 16, LANES)


    @pl.when(sums)
    def _():
        pl.semaphore_wait(barrier, expected)
        pl.semaphore_signal(go.at[0], inc=1, device_id=(partner, n), device_id_type=MESH)
        for other in range(narrows - 2):

            @pl.when(other + 1 < n)
            def _():
                pl.semaphore_signal(go.at[1], inc=1, device_id=(w, other), device_id_type=MESH)

    @pl.when(jnp.logical_not(sums))
    def _():
        pl.semaphore_wait(go.at[0], 1)

    edges = [
        (b_v.at[0], bb_v, jnp.logical_and(has_next, up), jnp.logical_and(has_prev, down), (w + 1, n - 1)),
        (b_v.at[rows + 1], bt_v, jnp.logical_and(has_next, down), jnp.logical_and(has_prev, up), (w + 1, n + 1)),
        (b_v.at[pl.ds(1, rows)], bm_v, has_next, has_prev, (w + 1, n)),
        (a_v.at[0], ab_v, up, down, (w, n - 1)),
        (a_v.at[rows + 1], at_v, down, up, (w, n + 1)),
    ]
    edge_copies = []
    for k, (src, dst, gives, gets, to) in enumerate(edges):
        copy = sent(src, dst, sh_sem.at[k], gh_sem.at[k], to)
        edge_copies.append(copy)

        @pl.when(gives)
        def _():
            copy.start()

        @pl.when(jnp.logical_not(gets))
        def _():
            dst[...] = jnp.zeros(dst.shape, F32)

    hi, lo = halves(weight - means)
    wst[:64] = hi
    wst[64:] = lo

    row16 = lax.broadcasted_iota(jnp.int32, (16, LANES), 0)

    @pl.when(sums)
    def _():
        pair_copy.wait_recv()
        for tile in range(30):
            total = part[tile] + pair[tile]
            if tile % 5 == 4:
                hi = total.astype(BF16).astype(F32)
                total = jnp.where(row16 < 2, hi, pltpu.roll(total - hi, 2, 0))
            share[tile % each // half, tile // each, tile % half] = total.astype(BF16)
        for tile in range(30, highs * each):
            share[tile % each // half, tile // each, tile % half] = jnp.zeros((16, LANES), BF16)
        for p in range(2):
            for i in range(1, highs):
                to = (chip_y + i) % highs
                sent(share.at[p, to], got1.at[p, i - 1], s1.at[p], g1.at[p], core1(to, chip_z)).start()

    def first_sums():
        for p in range(2):
            landed(got1.at[p], g1.at[p])
            total = share[p, chip_y].astype(F32)
            for i in range(1, highs):
                total = total + got1[p, i - 1].astype(F32)
            own32[p] = total
            own[p] = total.astype(BF16)
            for z in range(DEPTHS):

                @pl.when(z != chip_z)
                def _():
                    slot = lax.rem(z - chip_z + DEPTHS, DEPTHS) - 1
                    sent(own.at[p], got2.at[p, slot], s1.at[2 + p], g1.at[2 + p], core1(chip_y, z)).start()

    @pl.when(jnp.logical_and(sums, chip_z > 0))
    def _():
        first_sums()

    for k, (src, dst, gives, gets, to) in enumerate(edges):

        @pl.when(gets)
        def _():
            edge_copies[k].wait_recv()

    lane1 = lax.broadcasted_iota(jnp.int32, (16, LANES), 1)
    pick = jnp.where(
        (lax.broadcasted_iota(jnp.int32, (32, LANES), 1) % 64) // 2
        == lax.broadcasted_iota(jnp.int32, (32, LANES), 0),
        1.0,
        0.0,
    ).astype(BF16)
    latents = []
    for h in range(rows):
        value = a_v[h + 1] + bm_v[h]
        if h == 0:
            value = value + (at_v[...] + bt_v[...])
        if h == rows - 1:
            value = value + (ab_v[...] + bb_v[...])
        latents.append(value)
    patches = []
    for p in range(pairs):
        blocks = []
        for t in range(2):
            for u in range(2):
                for v in range(2):
                    keep = jnp.logical_and(lane1 // 64 == t, lane1 % 2 == v)
                    blocks.append(jnp.where(keep, latents[2 * p + u], 0.0).astype(BF16))
        patches.append(dot_t(pick, jnp.concatenate(blocks, axis=0)))
    x = jnp.concatenate(patches, axis=0)
    x_all[n] = x.astype(BF16)

    @pl.when(sums)
    def _():

        @pl.when(n < narrows - 2)
        def _():
            pl.semaphore_wait(go.at[1], narrows - 2 - n)

        pl.semaphore_signal(go.at[1], inc=1, device_id=(partner, n), device_id_type=MESH)

    @pl.when(jnp.logical_not(sums))
    def _():
        pl.semaphore_wait(go.at[1], 1)

    for i in range(1, narrows):
        sent(x_all.at[n], x_all.at[n], sx.at[0], gx.at[0], (w, (n + i) % narrows)).start()

    per = x.shape[0]
    other = rolled(x, 64)
    low = lax.broadcasted_iota(jnp.int32, x.shape, 1) < 64
    twice = jnp.concatenate([jnp.where(low, x, other), jnp.where(low, other, x)], axis=0).astype(BF16)
    squares = jnp.zeros((2 * per, LANES), F32)
    step = 512
    for k in range(width // step):
        piece = pl.ds(k * step, step)
        centre = dot(twice, wst[:, piece]) + (pb_v[:, piece] - bias_mean)
        centre = centre * centre
        for i in range(step // LANES):
            squares = squares + centre[:, i * LANES : (i + 1) * LANES]
    spread = jnp.sum(squares, axis=1, keepdims=True) * (1.0 / width)
    factor = lax.rsqrt(spread + 1e-06)
    lane2 = lax.broadcasted_iota(jnp.int32, (per, LANES), 1)
    placed = jnp.where(lane2 == 0, factor[:per], jnp.where(lane2 == 1, factor[per:], 0.0))
    placed = jnp.concatenate([placed, jnp.zeros((LANES - per, LANES), F32)], axis=0)
    r_all[n] = jnp.transpose(placed)[:8]
    for i in range(1, narrows):
        sent(r_all.at[n], r_all.at[n], sx.at[1], gx.at[1], (w, (n + i) % narrows)).start()

    @pl.when(jnp.logical_and(sums, chip_z == 0))
    def _():
        first_sums()

    @pl.when(sums)
    def _():
        for p in range(2):
            landed(got2.at[p], g1.at[2 + p])
            total = own32[p]
            for i in range(1, DEPTHS):
                total = total + got2[p, i - 1].astype(F32)
            for k in range(half):
                plain = total[k]
                both = plain + pltpu.roll(plain, 14, 0)
                hi = both.astype(BF16).astype(F32)
                both = jnp.where(row16 < 2, hi, pltpu.roll(both - hi, 2, 0))
                tile = each * chip_y + half * p + k
                m_all[tile] = jnp.where(tile % 5 == 4, both, plain).astype(BF16)
            mine = m_all.at[pl.ds(each * chip_y + half * p, half)]
            for c in reversed(range(CORES)):
                for y in range(highs):

                    @pl.when(jnp.logical_or(y != chip_y, c != core))
                    def _():
                        sent(mine, mine, s1.at[4], g1.at[4], at(y, chip_z, c)).start()


    loads[6].wait()
    loads[7].wait()
    e_out[0:3] = qb_v[...]
    e_out[3:5, :LANES] = ng_v[...]
    landed(x_all.at[pl.ds(0, narrows - 1)], gx.at[0])
    landed(r_all.at[pl.ds(0, narrows - 1)], gx.at[1])
    flat = r_all[...].reshape(narrows * 8, LANES)
    turned = jnp.transpose(jnp.concatenate([flat, jnp.zeros((LANES - narrows * 8, LANES), F32)], axis=0))
    for src in range(narrows):
        theirs = x_all[src].astype(F32)
        columns = [
            jnp.broadcast_to(turned[:per, 8 * src + t : 8 * src + t + 1], (per, LANES)) for t in range(2)
        ]
        value = theirs * jnp.where(low, columns[0], columns[1])
        hi = value.astype(BF16).astype(F32)
        lo = value - hi
        crossed = rolled(jnp.where(low, lo, hi), 64)
        values = [jnp.where(low, hi, crossed), jnp.where(low, crossed, lo)]
        for t in range(2):
            hi = columns[t].astype(BF16).astype(F32)
            more = jnp.where(lane2 == 1, columns[t] - hi, jnp.where(lane2 < 3, hi, 1.0))
            place = pl.ds((t * narrows + src) * per, per)
            x_out[place, :LANES] = values[t].astype(BF16)
            x_out[place, LANES:] = more.astype(BF16)
    @pl.when(sums)
    def _():
        landed(m_all.at[pl.ds(0, each * (highs - 1))], g1.at[4])

    @pl.when(jnp.logical_not(sums))
    def _():
        landed(m_all, g1.at[4])

    m_out[...] = m_all[...]
    landed(x_all.at[pl.ds(0, narrows - 1)], sx.at[0])
    landed(r_all.at[pl.ds(0, narrows - 1)], sx.at[1])

    @pl.when(sums)
    def _():
        for p in range(2):
            landed(got1.at[p], s1.at[p])
            landed(got2.at[p], s1.at[2 + p])
        landed(m_all, s1.at[4])
        landed(m_all.at[pl.ds(0, each * (highs - 1))], s1.at[4])

    @pl.when(jnp.logical_not(sums))
    def _():
        pair_copy.wait_send()

    for k, (src, dst, gives, gets, to) in enumerate(edges):

        @pl.when(gives)
        def _():
            edge_copies[k].wait_send()


def back(x_ref, m_ref, e_ref, out, mm, stage, sems):
    tokens = x_ref.shape[0] // 2
    row16 = lax.broadcasted_iota(jnp.int32, (16, LANES), 0)
    mm[144:] = jnp.zeros((112, 768), BF16)
    for head in range(2):
        for j in range(3):
            cols = slice(256 * j + LANES * head, 256 * j + LANES * (head + 1))
            tile = 15 * head + 5 * j
            block = m_ref[tile : tile + 4].reshape(64, LANES)
            mm[:64, cols] = block
            mm[64:128, cols] = block
            extra = m_ref[tile + 4].astype(F32)
            constant = extra[1:2] + extra[3:4] + e_ref[j : j + 1, LANES * head : LANES * (head + 1)]
            high = constant.astype(BF16).astype(F32)
            rows = jnp.where(row16 < 2, extra[0:1], 0.0)
            rows = jnp.where(row16 == 2, extra[2:3], rows)
            rows = jnp.where(row16 == 3, high, rows)
            rows = jnp.where(row16 == 4, constant - high, rows)
            mm[128:144, cols] = rows.astype(BF16)
    copies = []
    half = tokens // 2
    for part in range(4):
        for j in range(3):
            place = pl.ds(part * half, half)
            product = dot(x_ref[place], mm[:, 256 * j : 256 * j + 256])
            for hd in range(2):
                cols = slice(LANES * hd, LANES * hd + LANES)
                y = product[:, cols]
                if j < 2:
                    mean = jnp.sum(y * y, axis=1, keepdims=True) * (1.0 / LANES)
                    y = y * lax.rsqrt(mean + 1e-06) * e_ref[3 + j : 4 + j, :LANES]
                stage[j, place, cols] = y.astype(BF16)
            copy = pltpu.make_async_copy(stage.at[j, place], out.at[j, place], sems.at[3 * part + j])
            copy.start()
            copies.append(copy)
    for copy in copies:
        copy.wait()


def local(wides, narrows, activations, conv_weight, patch_weight, patch_bias, shift, scale, qkv_weight, qkv_bias, norm_gains):
    rows, cols, channels = activations.shape[1:]
    width = patch_weight.shape[1]
    taps = jnp.transpose(conv_weight, (0, 1, 2, 4, 3)).reshape(-1, channels)
    qkv = jnp.transpose(qkv_weight, (1, 0, 2))
    highs = wides // (CORES * DEPTHS)
    half = -(-30 // (2 * highs))
    per = rows // 2 * cols // 2
    any_spec = pl.BlockSpec(memory_space=pltpu.HBM)
    vmem = pl.BlockSpec(memory_space=pltpu.VMEM)
    dma = pltpu.SemaphoreType.DMA
    edge = pltpu.VMEM((16, LANES), F32)
    x, m, e = pl.pallas_call(
        functools.partial(front, (wides, narrows, rows, width)),
        out_shape=[
            jax.ShapeDtypeStruct((2 * narrows * per, 2 * LANES), BF16),
            jax.ShapeDtypeStruct((highs * 2 * half, 16, LANES), BF16),
            jax.ShapeDtypeStruct((8, 256), F32),
        ],
        in_specs=[any_spec] * 9,
        out_specs=[vmem] * 3,
        scratch_shapes=[
            pltpu.VMEM((rows, 2, cols, channels), BF16),
            pltpu.VMEM(taps.shape, BF16),
            pltpu.VMEM(patch_weight.shape, BF16),
            pltpu.VMEM((1, width), F32),
            pltpu.VMEM((1, width), F32),
            pltpu.VMEM((1, width), F32),
            pltpu.VMEM((3, LANES, 256), BF16),
            pltpu.VMEM(qkv_bias.shape, F32),
            pltpu.VMEM(norm_gains.shape, F32),
            pltpu.VMEM((30, 16, LANES), F32),
            pltpu.VMEM((30, 16, LANES), F32),
            pltpu.VMEM((2, highs, half, 16, LANES), BF16),
            pltpu.VMEM((2, highs - 1, half, 16, LANES), BF16),
            pltpu.VMEM((2, half, 16, LANES), BF16),
            pltpu.VMEM((2, half, 16, LANES), F32),
            pltpu.VMEM((2, DEPTHS - 1, half, 16, LANES), BF16),
            pltpu.VMEM((highs * 2 * half, 16, LANES), BF16),
            pltpu.VMEM((rows, taps.shape[0], LANES), F32),
            pltpu.VMEM((rows + 2, 16, LANES), F32),
            pltpu.VMEM((rows + 2, 16, LANES), F32),
            edge,
            edge,
            pltpu.VMEM((rows, 16, LANES), F32),
            edge,
            edge,
            pltpu.VMEM((LANES, width), BF16),
            pltpu.VMEM((narrows, per, LANES), BF16),
            pltpu.VMEM((narrows, 8, LANES), F32),
            dma((8,)),
            dma((rows // 2,)),
            pltpu.SemaphoreType.REGULAR((2,)),
            dma((1,)),
            dma((1,)),
            dma((5,)),
            dma((5,)),
            dma((2,)),
            dma((2,)),
            dma((5,)),
            dma((5,)),
        ],
        compiler_params=pltpu.CompilerParams(
            collective_id=0, has_side_effects=True, vmem_limit_bytes=40 * 1024 * 1024
        ),
        name="front",
    )(
        *(
            pltpu.with_memory_space_constraint(a, pltpu.HBM)
            for a in (
                activations,
                taps,
                patch_weight,
                patch_bias.reshape(1, -1),
                shift.reshape(1, -1),
                scale.reshape(1, -1),
                qkv,
                qkv_bias,
                norm_gains,
            )
        )
    )
    tokens = narrows * per
    return pl.pallas_call(
        back,
        out_shape=jax.ShapeDtypeStruct((3, 2 * tokens, 256), BF16),
        in_specs=[vmem] * 3,
        out_specs=any_spec,
        scratch_shapes=[
            pltpu.VMEM((2 * LANES, 768), BF16),
            pltpu.VMEM((3, 2 * tokens, 256), BF16),
            dma((12,)),
        ],
        compiler_params=pltpu.CompilerParams(vmem_limit_bytes=40 * 1024 * 1024),
        name="back",
    )(x, m, e)


def solution(mesh):
    placed = (
        P("wide", "narrow", None, None),
        P(),
        P(),
        P(),
        P(),
        P(),
        P("wide", None, "narrow"),
        P(None, "narrow"),
        P(),
    )
    return jax.shard_map(
        functools.partial(local, mesh.shape["wide"], mesh.shape["narrow"]),
        mesh=mesh,
        in_specs=placed,
        out_specs=P(None, "wide", "narrow"),
        check_vma=False,
    )
```

```python
import functools
import math

import jax
import jax.numpy as jnp
from jax import lax
from jax.experimental import pallas as pl
from jax.experimental.pallas import tpu as pltpu
from jax.sharding import PartitionSpec as P

MESH = pl.DeviceIdType.MESH
F32 = jnp.float32
BF16 = jnp.bfloat16
DEPTHS = 4
CORES = 2
LANES = 128


def rolled(x, by):
    return pltpu.roll(x, by % x.shape[1], 1)


def halves(x):
    high = x.astype(BF16)
    return high, (x - high.astype(F32)).astype(BF16)


def dot(a, b):
    return lax.dot_general(a, b, (((1,), (0,)), ((), ())), preferred_element_type=F32)


def dot_t(a, b):
    return lax.dot_general(a, b, (((1,), (1,)), ((), ())), preferred_element_type=F32)


def front(
    sizes,
    act, cw, pw, pb, sh, sc, qw, qb, ng,
    x_out, m_out, e_out,
    act_v, cw_v, pw_v, pb_v, sh_v, sc_v, qw_v, qb_v, ng_v,
    part, pair, share, got1, own, own32, got2, m_all, prod,
    a_v, b_v, at_v, ab_v, bm_v, bt_v, bb_v,
    wst, x_all, r_all,
    in_sem, go, out_sem, g0, g1, gx, gh_sem,
):
    wides, narrows, rows, width = sizes
    span = qw.shape[1]
    w = lax.axis_index("wide")
    n = lax.axis_index("narrow")
    pairs = rows // 2
    chips = wides // CORES
    core = w % CORES
    me = w // CORES
    partner = w + 1 - 2 * core
    sums = core == CORES - 1

    chip_y = me // DEPTHS
    chip_z = me % DEPTHS
    highs = chips // DEPTHS
    half = share.shape[2]
    each = 2 * half

    def at(y, z, c):
        return (y % highs * DEPTHS + z % DEPTHS) * CORES + c, n

    def core1(y, z):
        return at(y, z, CORES - 1)

    def landed(ref, sem):
        pltpu.make_async_copy(ref, ref, sem).wait()

    def lines(*refs):
        return sum(math.prod(ref.shape) * ref.dtype.itemsize for ref in refs) // (4 * LANES)

    def landed_lines(count, sem):
        planes = 4 if count % 4 == 0 and count // 4 <= prod.shape[1] else rows
        landed(prod.at[pl.ds(0, planes), pl.ds(0, count // planes)], sem)

    qw_part = qw_v.at[:, pl.ds(0, span), :]
    small = [(sc, sc_v), (sh, sh_v), (pb, pb_v), (qb, qb_v), (ng, ng_v)]
    pltpu.make_async_copy(pw, pw_v, in_sem.at[0]).start()
    for k, (src, dst) in enumerate(small[:3]):
        pltpu.make_async_copy(src, dst, in_sem.at[2 + k]).start()
    pltpu.make_async_copy(qw, qw_part, in_sem.at[0]).start()
    pltpu.make_async_copy(cw, cw_v, in_sem.at[1]).start()
    for t in range(2):
        pltpu.make_async_copy(act.at[t], act_v.at[:, t], in_sem.at[1]).start()
    for k, (src, dst) in enumerate(small[3:]):
        pltpu.make_async_copy(src, dst, in_sem.at[5 + k]).start()

    barrier = pltpu.get_barrier_semaphore()

    def greet(wide, narrow):
        pl.semaphore_signal(barrier, inc=1, device_id=(wide, narrow), device_id_type=MESH)

    has_next = w < wides - 1
    has_prev = w > 0
    up = n > 0
    down = n < narrows - 1
    for i in range(1, highs):
        greet(*core1(chip_y + i, chip_z))
    for other in range(narrows):

        @pl.when(jnp.logical_or(n < other, n == other + 1))
        def _():
            greet(w + CORES - 1 - core, other)

    greet(partner, n)

    @pl.when(sums)
    def _():
        for i in range(1, DEPTHS):
            greet(*core1(chip_y, chip_z + i))

        @pl.when(up)
        def _():
            greet(w, n - 1)

        @pl.when(down)
        def _():
            greet(w, n + 1)

    @pl.when(jnp.logical_and(jnp.logical_not(sums), has_prev))
    def _():
        greet(w - 1, n)

        @pl.when(up)
        def _():
            greet(w - 1, n - 1)

        @pl.when(down)
        def _():
            greet(w - 1, n + 1)

    across = jnp.where(up, 1, 0) + jnp.where(down, 1, 0)
    expected = CORES * (n + jnp.where(down, 1, 0)) + across + jnp.where(has_next, 1 + across, 0) + CORES * (highs - 1) + DEPTHS

    qw_v[:, span:, :] = jnp.zeros((3, qw_v.shape[1] - span, qw_v.shape[2]), BF16)
    landed_lines(lines(pw_v, qw_part), in_sem.at[0])
    for k in range(3):
        landed(small[k][1], in_sem.at[2 + k])
    weight = pw_v[...].astype(F32)
    means = jnp.sum(weight, axis=1, keepdims=True) * (1.0 / width)
    bias_mean = jnp.sum(pb_v[...], axis=1, keepdims=True) * (1.0 / width)
    begin = w * span
    base = pl.multiple_of(jnp.minimum(begin // LANES, width // LANES - 2) * LANES, LANES)
    window = pl.ds(base, 2 * LANES)
    gain = 1.0 + sc_v[:, window]
    main = (pw_v[:, window].astype(F32) - means) * gain
    extra_b = (pb_v[:, window] - bias_mean) * gain
    extra_s = sh_v[:, window]
    pad = jnp.zeros((14, 2 * LANES), F32)
    stacked = jnp.concatenate([main, extra_b, extra_s, pad], axis=0)
    shift_by = (2 * LANES - (begin - base)) % (2 * LANES)
    stacked = pltpu.roll(stacked, shift_by, 1)[:, :LANES]
    lane = lax.broadcasted_iota(jnp.int32, stacked.shape, 1)
    stacked = jnp.where(lane < span, stacked, 0.0)
    hi, lo = halves(stacked)
    for j in range(3):
        res = dot(hi, qw_v[j]) + dot(lo, qw_v[j])
        for head in range(2):
            part[15 * head + 5 * j : 15 * head + 5 * j + 5] = res[:, head * LANES : (head + 1) * LANES].reshape(5, 16, LANES)
    def sent(src, dst, ssem, gsem, to):
        return pltpu.make_async_remote_copy(
            src_ref=src, dst_ref=dst, send_sem=ssem, recv_sem=gsem, device_id=to, device_id_type=MESH
        )

    pair_copy = sent(part, pair, out_sem.at[0], g0.at[0], (partner, n))

    @pl.when(jnp.logical_not(sums))
    def _():
        pl.semaphore_wait(barrier, 1)
        pair_copy.start()

    landed_lines(lines(cw_v, act_v), in_sem.at[1])
    for k in range(pairs):
        raw = act_v[2 * k : 2 * k + 2].reshape(256, act.shape[3]).astype(F32)
        less = 0.5 * raw
        acted = (less + less * jnp.tanh(less)).astype(BF16)
        res = dot_t(cw_v[...], acted)
        prod[2 * k] = res[:, :LANES]
        prod[2 * k + 1] = res[:, LANES:]

    full = (16 * (rows + 2), LANES)
    col = lax.broadcasted_iota(jnp.int32, full, 1) % 64
    early = lax.broadcasted_iota(jnp.int32, full, 1) < 64
    taps = []
    for a in range(3):
        moved = []
        for c in range(3):
            planes = []
            for h in range(-1, rows + 1):
                total = None
                for b in range(3):
                    src = h + b - 1
                    if 0 <= src < rows:
                        g = (a * 3 + b) * 3 + c
                        piece = prod[src, 16 * g : 16 * g + 16, :]
                        total = piece if total is None else total + piece
                planes.append(total)
            moved.append(jnp.concatenate(planes, axis=0))
        left = jnp.where(col == 0, 0.0, rolled(moved[0], 1))
        right = jnp.where(col == 63, 0.0, rolled(moved[2], -1))
        taps.append(moved[1] + left + right)
    swapped = rolled(taps[1], 64)
    here = taps[2] + jnp.where(early, 0.0, swapped)
    ahead = taps[0] + jnp.where(early, swapped, 0.0)
    copies = jnp.where(early, taps[1] + taps[0], rolled(taps[0], 64))
    here = here + jnp.where(w == 0, copies, 0.0)
    a_v[...] = here.reshape(rows + 2, 16, LANES)
    b_v[...] = ahead.reshape(rows + 2, 16, LANES)


    @pl.when(sums)
    def _():
        pl.semaphore_wait(barrier, expected)
        pl.semaphore_signal(go.at[0], inc=1, device_id=(partner, n), device_id_type=MESH)
        for other in range(narrows - 2):

            @pl.when(other + 1 < n)
            def _():
                pl.semaphore_signal(go.at[1], inc=1, device_id=(w, other), device_id_type=MESH)

    @pl.when(jnp.logical_not(sums))
    def _():
        pl.semaphore_wait(go.at[0], 1)

    edges = [
        (b_v.at[0], bb_v, jnp.logical_and(has_next, up), jnp.logical_and(has_prev, down), (w + 1, n - 1)),
        (b_v.at[rows + 1], bt_v, jnp.logical_and(has_next, down), jnp.logical_and(has_prev, up), (w + 1, n + 1)),
        (b_v.at[pl.ds(1, rows)], bm_v, has_next, has_prev, (w + 1, n)),
        (a_v.at[0], ab_v, up, down, (w, n - 1)),
        (a_v.at[rows + 1], at_v, down, up, (w, n + 1)),
    ]
    edge_copies = []
    for k, (src, dst, gives, gets, to) in enumerate(edges):
        copy = sent(src, dst, out_sem.at[0], gh_sem.at[0], to)
        edge_copies.append(copy)

        @pl.when(gives)
        def _():
            copy.start()

        @pl.when(jnp.logical_not(gets))
        def _():
            dst[...] = jnp.zeros(dst.shape, F32)

    row16 = lax.broadcasted_iota(jnp.int32, (16, LANES), 0)

    @pl.when(sums)
    def _():
        pair_copy.wait_recv()
        for tile in range(30):
            total = part[tile] + pair[tile]
            if tile % 5 == 4:
                hi = total.astype(BF16).astype(F32)
                total = jnp.where(row16 < 2, hi, pltpu.roll(total - hi, 2, 0))
            share[tile % each // half, tile // each, tile % half] = total.astype(BF16)
        for tile in range(30, highs * each):
            share[tile % each // half, tile // each, tile % half] = jnp.zeros((16, LANES), BF16)
        for p in range(2):
            for i in range(1, highs):
                to = (chip_y + i) % highs
                sent(share.at[p, to], got1.at[p, i - 1], out_sem.at[0], g1.at[p], core1(to, chip_z)).start()

    hi, lo = halves(weight - means)
    wst[:64] = hi
    wst[64:] = lo

    def first_sums():
        for p in range(2):
            landed(got1.at[p], g1.at[p])
            total = share[p, chip_y].astype(F32)
            for i in range(1, highs):
                total = total + got1[p, i - 1].astype(F32)
            own32[p] = total
            own[p] = total.astype(BF16)
            for z in range(DEPTHS):

                @pl.when(z != chip_z)
                def _():
                    slot = lax.rem(z - chip_z + DEPTHS, DEPTHS) - 1
                    sent(own.at[p], got2.at[p, slot], out_sem.at[0], g1.at[2 + p], core1(chip_y, z)).start()

    @pl.when(jnp.logical_and(sums, chip_z > 0))
    def _():
        first_sums()

    edge = lines(a_v.at[0])
    main = lines(bm_v)
    beside = jnp.where(up, 1, 0) + jnp.where(down, 1, 0)
    for sides in (1, 2):

        @pl.when(jnp.logical_and(beside == sides, has_prev))
        def _():
            landed_lines(main + 2 * sides * edge, gh_sem.at[0])

        @pl.when(jnp.logical_and(beside == sides, jnp.logical_not(has_prev)))
        def _():
            landed_lines(sides * edge, gh_sem.at[0])

    lane1 = lax.broadcasted_iota(jnp.int32, (16, LANES), 1)
    pick = jnp.where(
        (lax.broadcasted_iota(jnp.int32, (32, LANES), 1) % 64) // 2
        == lax.broadcasted_iota(jnp.int32, (32, LANES), 0),
        1.0,
        0.0,
    ).astype(BF16)
    latents = []
    for h in range(rows):
        value = a_v[h + 1] + bm_v[h]
        if h == 0:
            value = value + (at_v[...] + bt_v[...])
        if h == rows - 1:
            value = value + (ab_v[...] + bb_v[...])
        latents.append(value)
    patches = []
    for p in range(pairs):
        blocks = []
        for t in range(2):
            for u in range(2):
                for v in range(2):
                    keep = jnp.logical_and(lane1 // 64 == t, lane1 % 2 == v)
                    blocks.append(jnp.where(keep, latents[2 * p + u], 0.0).astype(BF16))
        patches.append(dot_t(pick, jnp.concatenate(blocks, axis=0)))
    x = jnp.concatenate(patches, axis=0)
    x_all[n] = x.astype(BF16)

    @pl.when(sums)
    def _():

        @pl.when(n < narrows - 2)
        def _():
            pl.semaphore_wait(go.at[1], narrows - 2 - n)

        pl.semaphore_signal(go.at[1], inc=1, device_id=(partner, n), device_id_type=MESH)

    @pl.when(jnp.logical_not(sums))
    def _():
        pl.semaphore_wait(go.at[1], 1)

    for i in range(1, narrows):
        sent(x_all.at[n], x_all.at[n], out_sem.at[0], gx.at[0], (w, (n + i) % narrows)).start()

    per = x.shape[0]
    other = rolled(x, 64)
    low = lax.broadcasted_iota(jnp.int32, x.shape, 1) < 64
    twice = jnp.concatenate([jnp.where(low, x, other), jnp.where(low, other, x)], axis=0).astype(BF16)
    squares = jnp.zeros((2 * per, LANES), F32)
    step = 512
    for k in range(width // step):
        piece = pl.ds(k * step, step)
        centre = dot(twice, wst[:, piece]) + (pb_v[:, piece] - bias_mean)
        centre = centre * centre
        for i in range(step // LANES):
            squares = squares + centre[:, i * LANES : (i + 1) * LANES]
    spread = jnp.sum(squares, axis=1, keepdims=True) * (1.0 / width)
    factor = lax.rsqrt(spread + 1e-06)
    lane2 = lax.broadcasted_iota(jnp.int32, (per, LANES), 1)
    chosen = jnp.where(lane2 < 3, factor[:per], factor[per:])
    hi = chosen.astype(BF16).astype(F32)
    mid = (chosen - hi).astype(BF16).astype(F32)
    chosen = jnp.where(lane2 % 3 == 0, hi, jnp.where(lane2 % 3 == 1, mid, chosen - hi - mid))
    placed = jnp.where(lane2 < 6, chosen, jnp.where(lane2 == 6, 1.0, 0.0))
    placed = jnp.concatenate([placed, jnp.zeros((LANES - per, LANES), F32)], axis=0)
    r_all[n] = jnp.transpose(placed)[:16].astype(BF16)
    for i in range(1, narrows):
        sent(r_all.at[n], r_all.at[n], out_sem.at[0], gx.at[1], (w, (n + i) % narrows)).start()

    @pl.when(jnp.logical_and(sums, chip_z == 0))
    def _():
        first_sums()

    @pl.when(sums)
    def _():
        for p in range(2):
            landed(got2.at[p], g1.at[2 + p])
            total = own32[p]
            for i in range(1, DEPTHS):
                total = total + got2[p, i - 1].astype(F32)
            for k in range(half):
                plain = total[k]
                both = plain + pltpu.roll(plain, 14, 0)
                hi = both.astype(BF16).astype(F32)
                both = jnp.where(row16 < 2, hi, pltpu.roll(both - hi, 2, 0))
                tile = each * chip_y + half * p + k
                m_all[tile] = jnp.where(tile % 5 == 4, both, plain).astype(BF16)
            mine = m_all.at[pl.ds(each * chip_y + half * p, half)]
            for c in reversed(range(CORES)):
                for y in range(highs):

                    @pl.when(jnp.logical_or(y != chip_y, c != core))
                    def _():
                        sent(mine, mine, out_sem.at[0], g1.at[4], at(y, chip_z, c)).start()


    landed(qb_v, in_sem.at[5])
    landed(ng_v, in_sem.at[6])
    e_out[0:3] = qb_v[...]
    e_out[3:5, :LANES] = ng_v[...]
    landed(x_all.at[pl.ds(0, narrows - 1)], gx.at[0])
    landed(r_all.at[pl.ds(0, narrows - 1)], gx.at[1])
    term = lax.broadcasted_iota(jnp.int32, (16, 3 * LANES), 0)
    place = lax.broadcasted_iota(jnp.int32, (16, 3 * LANES), 1)
    spot = place % LANES
    frame = jnp.where(place < LANES, spot // 64, place // LANES - 1)
    wanted = jnp.where(place < LANES, 0, jnp.where(spot < 3, 1, jnp.where(spot < 5, 2, 3)))
    taken = (wanted == 0) & (term // 3 == frame)
    taken = taken | ((wanted == 1) & (term == 3 * frame + spot % 2)) | ((wanted == 2) & (term == 6))
    spread_out = jnp.where(taken, 1.0, 0.0).astype(BF16)
    for src in range(narrows):
        table = lax.dot_general(
            r_all[src], spread_out, (((0,), (0,)), ((), ())), preferred_element_type=F32
        )[:per]
        value = x_all[src].astype(F32) * table[:, :LANES]
        hi = value.astype(BF16).astype(F32)
        lo = value - hi
        crossed = rolled(jnp.where(low, lo, hi), 64)
        values = [jnp.where(low, hi, crossed), jnp.where(low, crossed, lo)]
        for t in range(2):
            place = pl.ds((t * narrows + src) * per, per)
            x_out[place, :LANES] = values[t].astype(BF16)
            x_out[place, LANES:] = table[:, LANES * (t + 1) : LANES * (t + 2)].astype(BF16)
    @pl.when(sums)
    def _():
        landed(m_all.at[pl.ds(0, each * (highs - 1))], g1.at[4])

    @pl.when(jnp.logical_not(sums))
    def _():
        landed(m_all, g1.at[4])

    m_out[...] = m_all[...]
    always = (narrows - 1) * (lines(x_all) + lines(r_all)) // narrows
    spread_lines = (CORES * highs - 1) * lines(m_all) // highs
    for sides in (1, 2):
        for follows in (False, True):
            for adds in (False, True):
                gone = always + sides * edge + (main + sides * edge if follows else 0)
                gone += lines(got1, got2) + spread_lines if adds else lines(part)
                here_so = jnp.logical_and(beside == sides, has_next == follows)

                @pl.when(jnp.logical_and(here_so, sums == adds))
                def _():
                    landed_lines(gone, out_sem.at[0])


def back(x_ref, m_ref, e_ref, out, mm, stage, sems):
    tokens = x_ref.shape[0] // 2
    row16 = lax.broadcasted_iota(jnp.int32, (16, LANES), 0)
    mm[144:] = jnp.zeros((112, 768), BF16)
    for head in range(2):
        for j in range(3):
            cols = slice(256 * j + LANES * head, 256 * j + LANES * (head + 1))
            tile = 15 * head + 5 * j
            block = m_ref[tile : tile + 4].reshape(64, LANES)
            mm[:64, cols] = block
            mm[64:128, cols] = block
            extra = m_ref[tile + 4].astype(F32)
            constant = extra[1:2] + extra[3:4] + e_ref[j : j + 1, LANES * head : LANES * (head + 1)]
            high = constant.astype(BF16).astype(F32)
            rows = jnp.where(row16 < 2, extra[0:1], 0.0)
            rows = jnp.where(row16 == 2, extra[2:3], rows)
            rows = jnp.where(row16 == 3, high, rows)
            rows = jnp.where(row16 == 4, constant - high, rows)
            mm[128:144, cols] = rows.astype(BF16)
    half = tokens // 2
    for part in range(4):
        for j in range(3):
            place = pl.ds(part * half, half)
            product = dot(x_ref[place], mm[:, 256 * j : 256 * j + 256])
            for hd in range(2):
                cols = slice(LANES * hd, LANES * hd + LANES)
                y = product[:, cols]
                if j < 2:
                    mean = jnp.sum(y * y, axis=1, keepdims=True) * (1.0 / LANES)
                    y = y * lax.rsqrt(mean + 1e-06) * e_ref[3 + j : 4 + j, :LANES]
                stage[j, place, cols] = y.astype(BF16)
            copy = pltpu.make_async_copy(stage.at[j, place], out.at[j, place], sems.at[0])
            copy.start()
    pltpu.make_async_copy(stage, out, sems.at[0]).wait()


def local(wides, narrows, activations, conv_weight, patch_weight, patch_bias, shift, scale, qkv_weight, qkv_bias, norm_gains):
    rows, cols, channels = activations.shape[1:]
    width = patch_weight.shape[1]
    taps = jnp.transpose(conv_weight, (0, 1, 2, 4, 3)).reshape(-1, channels)
    qkv = jnp.transpose(qkv_weight, (1, 0, 2))
    highs = wides // (CORES * DEPTHS)
    half = -(-30 // (2 * highs))
    per = rows // 2 * cols // 2
    any_spec = pl.BlockSpec(memory_space=pltpu.HBM)
    vmem = pl.BlockSpec(memory_space=pltpu.VMEM)
    dma = pltpu.SemaphoreType.DMA
    edge = pltpu.VMEM((16, LANES), F32)
    x, m, e = pl.pallas_call(
        functools.partial(front, (wides, narrows, rows, width)),
        out_shape=[
            jax.ShapeDtypeStruct((2 * narrows * per, 2 * LANES), BF16),
            jax.ShapeDtypeStruct((highs * 2 * half, 16, LANES), BF16),
            jax.ShapeDtypeStruct((8, 256), F32),
        ],
        in_specs=[any_spec] * 9,
        out_specs=[vmem] * 3,
        scratch_shapes=[
            pltpu.VMEM((rows, 2, cols, channels), BF16),
            pltpu.VMEM(taps.shape, BF16),
            pltpu.VMEM(patch_weight.shape, BF16),
            pltpu.VMEM((1, width), F32),
            pltpu.VMEM((1, width), F32),
            pltpu.VMEM((1, width), F32),
            pltpu.VMEM((3, LANES, 256), BF16),
            pltpu.VMEM(qkv_bias.shape, F32),
            pltpu.VMEM(norm_gains.shape, F32),
            pltpu.VMEM((30, 16, LANES), F32),
            pltpu.VMEM((30, 16, LANES), F32),
            pltpu.VMEM((2, highs, half, 16, LANES), BF16),
            pltpu.VMEM((2, highs - 1, half, 16, LANES), BF16),
            pltpu.VMEM((2, half, 16, LANES), BF16),
            pltpu.VMEM((2, half, 16, LANES), F32),
            pltpu.VMEM((2, DEPTHS - 1, half, 16, LANES), BF16),
            pltpu.VMEM((highs * 2 * half, 16, LANES), BF16),
            pltpu.VMEM((rows, taps.shape[0], LANES), F32),
            pltpu.VMEM((rows + 2, 16, LANES), F32),
            pltpu.VMEM((rows + 2, 16, LANES), F32),
            edge,
            edge,
            pltpu.VMEM((rows, 16, LANES), F32),
            edge,
            edge,
            pltpu.VMEM((LANES, width), BF16),
            pltpu.VMEM((narrows, per, LANES), BF16),
            pltpu.VMEM((narrows, 16, LANES), BF16),
            dma((7,)),
            pltpu.SemaphoreType.REGULAR((2,)),
            dma((1,)),
            dma((1,)),
            dma((5,)),
            dma((2,)),
            dma((1,)),
        ],
        compiler_params=pltpu.CompilerParams(
            collective_id=0, has_side_effects=True, vmem_limit_bytes=40 * 1024 * 1024
        ),
        name="front",
    )(
        *(
            pltpu.with_memory_space_constraint(a, pltpu.HBM)
            for a in (
                activations,
                taps,
                patch_weight,
                patch_bias.reshape(1, -1),
                shift.reshape(1, -1),
                scale.reshape(1, -1),
                qkv,
                qkv_bias,
                norm_gains,
            )
        )
    )
    tokens = narrows * per
    return pl.pallas_call(
        back,
        out_shape=jax.ShapeDtypeStruct((3, 2 * tokens, 256), BF16),
        in_specs=[vmem] * 3,
        out_specs=any_spec,
        scratch_shapes=[
            pltpu.VMEM((2 * LANES, 768), BF16),
            pltpu.VMEM((3, 2 * tokens, 256), BF16),
            dma((1,)),
        ],
        compiler_params=pltpu.CompilerParams(vmem_limit_bytes=40 * 1024 * 1024),
        name="back",
    )(x, m, e)


def solution(mesh):
    placed = (
        P("wide", "narrow", None, None),
        P(),
        P(),
        P(),
        P(),
        P(),
        P("wide", None, "narrow"),
        P(None, "narrow"),
        P(),
    )
    return jax.shard_map(
        functools.partial(local, mesh.shape["wide"], mesh.shape["narrow"]),
        mesh=mesh,
        in_specs=placed,
        out_specs=P(None, "wide", "narrow"),
        check_vma=False,
    )
```

```python
import functools
import math

import jax
import jax.numpy as jnp
from jax import lax
from jax.experimental import pallas as pl
from jax.experimental.pallas import tpu as pltpu
from jax.sharding import PartitionSpec as P

MESH = pl.DeviceIdType.MESH
F32 = jnp.float32
BF16 = jnp.bfloat16
DEPTHS = 4
CORES = 2
LANES = 128


def rolled(x, by):
    return pltpu.roll(x, by % x.shape[1], 1)


def halves(x):
    high = x.astype(BF16)
    return high, (x - high.astype(F32)).astype(BF16)


def dot(a, b):
    return lax.dot_general(a, b, (((1,), (0,)), ((), ())), preferred_element_type=F32)


def dot_t(a, b):
    return lax.dot_general(a, b, (((1,), (1,)), ((), ())), preferred_element_type=F32)


def front(
    sizes,
    act, cw, pw, pb, sh, sc, qw, qb, ng,
    x_out, m_out, e_out,
    act_v, cw_v, pw_v, pb_v, sh_v, sc_v, qw_v, qb_v, ng_v,
    part, pair, share, got1, own, own32, got2, m_all, prod,
    a_v, b_v, at_v, ab_v, bm_v, bt_v, bb_v,
    wst, x_all, r_all,
    in_sem, go, out_sem, g0, g1, gx, gh_sem,
):
    wides, narrows, rows, width = sizes
    span = qw.shape[1]
    w = lax.axis_index("wide")
    n = lax.axis_index("narrow")
    pairs = rows // 2
    chips = wides // CORES
    core = w % CORES
    me = w // CORES
    partner = w + 1 - 2 * core
    sums = core == CORES - 1

    chip_y = me // DEPTHS
    chip_z = me % DEPTHS
    highs = chips // DEPTHS
    half = share.shape[2]
    each = 2 * half

    def at(y, z, c):
        return (y % highs * DEPTHS + z % DEPTHS) * CORES + c, n

    def core1(y, z):
        return at(y, z, CORES - 1)

    def landed(ref, sem):
        pltpu.make_async_copy(ref, ref, sem).wait()

    def lines(*refs):
        return sum(math.prod(ref.shape) * ref.dtype.itemsize for ref in refs) // (4 * LANES)

    def landed_lines(count, sem):
        planes = 4 if count % 4 == 0 and count // 4 <= prod.shape[1] else rows
        landed(prod.at[pl.ds(0, planes), pl.ds(0, count // planes)], sem)

    qw_part = qw_v.at[:, pl.ds(0, span), :]
    small = [(sc, sc_v), (sh, sh_v), (pb, pb_v), (qb, qb_v), (ng, ng_v)]
    pltpu.make_async_copy(pw, pw_v, in_sem.at[0]).start()
    for k, (src, dst) in enumerate(small[:3]):
        pltpu.make_async_copy(src, dst, in_sem.at[2 + k]).start()
    pltpu.make_async_copy(qw, qw_part, in_sem.at[0]).start()
    pltpu.make_async_copy(cw, cw_v, in_sem.at[1]).start()
    for t in range(2):
        pltpu.make_async_copy(act.at[t], act_v.at[:, t], in_sem.at[1]).start()
    for k, (src, dst) in enumerate(small[3:]):
        pltpu.make_async_copy(src, dst, in_sem.at[5 + k]).start()

    barrier = pltpu.get_barrier_semaphore()

    def greet(wide, narrow):
        pl.semaphore_signal(barrier, inc=1, device_id=(wide, narrow), device_id_type=MESH)

    has_next = w < wides - 1
    has_prev = w > 0
    up = n > 0
    down = n < narrows - 1
    for i in range(1, highs):
        greet(*core1(chip_y + i, chip_z))
    for other in range(narrows):

        @pl.when(jnp.logical_or(n < other, n == other + 1))
        def _():
            greet(w + CORES - 1 - core, other)

    greet(partner, n)

    @pl.when(sums)
    def _():
        for i in range(1, DEPTHS):
            greet(*core1(chip_y, chip_z + i))

        @pl.when(up)
        def _():
            greet(w, n - 1)

        @pl.when(down)
        def _():
            greet(w, n + 1)

    @pl.when(jnp.logical_and(jnp.logical_not(sums), has_prev))
    def _():
        greet(w - 1, n)

        @pl.when(up)
        def _():
            greet(w - 1, n - 1)

        @pl.when(down)
        def _():
            greet(w - 1, n + 1)

    across = jnp.where(up, 1, 0) + jnp.where(down, 1, 0)
    expected = CORES * (n + jnp.where(down, 1, 0)) + across + jnp.where(has_next, 1 + across, 0) + CORES * (highs - 1) + DEPTHS

    qw_v[:, span:, :] = jnp.zeros((3, qw_v.shape[1] - span, qw_v.shape[2]), BF16)
    landed_lines(lines(pw_v, qw_part), in_sem.at[0])
    for k in range(3):
        landed(small[k][1], in_sem.at[2 + k])
    weight = pw_v[...].astype(F32)
    means = jnp.sum(weight, axis=1, keepdims=True) * (1.0 / width)
    bias_mean = jnp.sum(pb_v[...], axis=1, keepdims=True) * (1.0 / width)
    begin = w * span
    base = pl.multiple_of(jnp.minimum(begin // LANES, width // LANES - 2) * LANES, LANES)
    window = pl.ds(base, 2 * LANES)
    gain = 1.0 + sc_v[:, window]
    main = (pw_v[:, window].astype(F32) - means) * gain
    extra_b = (pb_v[:, window] - bias_mean) * gain
    extra_s = sh_v[:, window]
    pad = jnp.zeros((14, 2 * LANES), F32)
    stacked = jnp.concatenate([main, extra_b, extra_s, pad], axis=0)
    shift_by = (2 * LANES - (begin - base)) % (2 * LANES)
    stacked = pltpu.roll(stacked, shift_by, 1)[:, :LANES]
    lane = lax.broadcasted_iota(jnp.int32, stacked.shape, 1)
    stacked = jnp.where(lane < span, stacked, 0.0)
    hi, lo = halves(stacked)
    for j in range(3):
        res = dot(hi, qw_v[j]) + dot(lo, qw_v[j])
        for head in range(2):
            part[15 * head + 5 * j : 15 * head + 5 * j + 5] = res[:, head * LANES : (head + 1) * LANES].reshape(5, 16, LANES)
    def sent(src, dst, ssem, gsem, to):
        return pltpu.make_async_remote_copy(
            src_ref=src, dst_ref=dst, send_sem=ssem, recv_sem=gsem, device_id=to, device_id_type=MESH
        )

    pair_copy = sent(part, pair, out_sem.at[0], g0.at[0], (partner, n))

    @pl.when(jnp.logical_not(sums))
    def _():
        pl.semaphore_wait(barrier, 1)
        pair_copy.start()

    landed_lines(lines(cw_v, act_v), in_sem.at[1])
    for k in range(pairs):
        raw = act_v[2 * k : 2 * k + 2].reshape(256, act.shape[3]).astype(F32)
        less = 0.5 * raw
        acted = (less + less * jnp.tanh(less)).astype(BF16)
        res = dot_t(cw_v[...], acted)
        prod[2 * k] = res[:, :LANES]
        prod[2 * k + 1] = res[:, LANES:]

    full = (16 * (rows + 2), LANES)
    col = lax.broadcasted_iota(jnp.int32, full, 1) % 64
    early = lax.broadcasted_iota(jnp.int32, full, 1) < 64
    taps = []
    for a in range(3):
        moved = []
        for c in range(3):
            planes = []
            for h in range(-1, rows + 1):
                total = None
                for b in range(3):
                    src = h + b - 1
                    if 0 <= src < rows:
                        g = (a * 3 + b) * 3 + c
                        piece = prod[src, 16 * g : 16 * g + 16, :]
                        total = piece if total is None else total + piece
                planes.append(total)
            moved.append(jnp.concatenate(planes, axis=0))
        left = jnp.where(col == 0, 0.0, rolled(moved[0], 1))
        right = jnp.where(col == 63, 0.0, rolled(moved[2], -1))
        taps.append(moved[1] + left + right)
    swapped = rolled(taps[1], 64)
    here = taps[2] + jnp.where(early, 0.0, swapped)
    ahead = taps[0] + jnp.where(early, swapped, 0.0)
    copies = jnp.where(early, taps[1] + taps[0], rolled(taps[0], 64))
    here = here + jnp.where(w == 0, copies, 0.0)
    a_v[...] = here.reshape(rows + 2, 16, LANES)
    b_v[...] = ahead.reshape(rows + 2, 16, LANES)


    @pl.when(sums)
    def _():
        pl.semaphore_wait(barrier, expected)
        pl.semaphore_signal(go.at[0], inc=1, device_id=(partner, n), device_id_type=MESH)
        for other in range(narrows - 2):

            @pl.when(other + 1 < n)
            def _():
                pl.semaphore_signal(go.at[1], inc=1, device_id=(w, other), device_id_type=MESH)

    @pl.when(jnp.logical_not(sums))
    def _():
        pl.semaphore_wait(go.at[0], 1)

    edges = [
        (b_v.at[0], bb_v, jnp.logical_and(has_next, up), jnp.logical_and(has_prev, down), (w + 1, n - 1)),
        (b_v.at[rows + 1], bt_v, jnp.logical_and(has_next, down), jnp.logical_and(has_prev, up), (w + 1, n + 1)),
        (b_v.at[pl.ds(1, rows)], bm_v, has_next, has_prev, (w + 1, n)),
        (a_v.at[0], ab_v, up, down, (w, n - 1)),
        (a_v.at[rows + 1], at_v, down, up, (w, n + 1)),
    ]
    edge_copies = []
    for k, (src, dst, gives, gets, to) in enumerate(edges):
        copy = sent(src, dst, out_sem.at[0], gh_sem.at[0], to)
        edge_copies.append(copy)

        @pl.when(gives)
        def _():
            copy.start()

        @pl.when(jnp.logical_not(gets))
        def _():
            dst[...] = jnp.zeros(dst.shape, F32)

    row16 = lax.broadcasted_iota(jnp.int32, (16, LANES), 0)

    @pl.when(sums)
    def _():
        pair_copy.wait_recv()
        for tile in range(30):
            total = part[tile] + pair[tile]
            if tile % 5 == 4:
                hi = total.astype(BF16).astype(F32)
                total = jnp.where(row16 < 2, hi, pltpu.roll(total - hi, 2, 0))
            share[tile % each // half, tile // each, tile % half] = total.astype(BF16)
        for tile in range(30, highs * each):
            share[tile % each // half, tile // each, tile % half] = jnp.zeros((16, LANES), BF16)
        for p in range(2):
            for i in range(1, highs):
                to = (chip_y + i) % highs
                sent(share.at[p, to], got1.at[p, i - 1], out_sem.at[0], g1.at[p], core1(to, chip_z)).start()

    hi, lo = halves(weight - means)
    wst[:64] = hi
    wst[64:] = lo

    def first_sums():
        for p in range(2):
            landed(got1.at[p], g1.at[p])
            total = share[p, chip_y].astype(F32)
            for i in range(1, highs):
                total = total + got1[p, i - 1].astype(F32)
            own32[p] = total
            own[p] = total.astype(BF16)
            for z in range(DEPTHS):

                @pl.when(z != chip_z)
                def _():
                    slot = lax.rem(z - chip_z + DEPTHS, DEPTHS) - 1
                    sent(own.at[p], got2.at[p, slot], out_sem.at[0], g1.at[2 + p], core1(chip_y, z)).start()

    @pl.when(jnp.logical_and(sums, chip_z > 0))
    def _():
        first_sums()

    edge = lines(a_v.at[0])
    main = lines(bm_v)
    beside = jnp.where(up, 1, 0) + jnp.where(down, 1, 0)
    for sides in (1, 2):

        @pl.when(jnp.logical_and(beside == sides, has_prev))
        def _():
            landed_lines(main + 2 * sides * edge, gh_sem.at[0])

        @pl.when(jnp.logical_and(beside == sides, jnp.logical_not(has_prev)))
        def _():
            landed_lines(sides * edge, gh_sem.at[0])

    lane1 = lax.broadcasted_iota(jnp.int32, (16, LANES), 1)
    pick = jnp.where(
        (lax.broadcasted_iota(jnp.int32, (32, LANES), 1) % 64) // 2
        == lax.broadcasted_iota(jnp.int32, (32, LANES), 0),
        1.0,
        0.0,
    ).astype(BF16)
    latents = []
    for h in range(rows):
        value = a_v[h + 1] + bm_v[h]
        if h == 0:
            value = value + (at_v[...] + bt_v[...])
        if h == rows - 1:
            value = value + (ab_v[...] + bb_v[...])
        latents.append(value)
    patches = []
    for p in range(pairs):
        blocks = []
        for t in range(2):
            for u in range(2):
                for v in range(2):
                    keep = jnp.logical_and(lane1 // 64 == t, lane1 % 2 == v)
                    blocks.append(jnp.where(keep, latents[2 * p + u], 0.0).astype(BF16))
        patches.append(dot_t(pick, jnp.concatenate(blocks, axis=0)))
    x = jnp.concatenate(patches, axis=0)
    x_all[n] = x.astype(BF16)

    @pl.when(sums)
    def _():

        @pl.when(n < narrows - 2)
        def _():
            pl.semaphore_wait(go.at[1], narrows - 2 - n)

        pl.semaphore_signal(go.at[1], inc=1, device_id=(partner, n), device_id_type=MESH)

    @pl.when(jnp.logical_not(sums))
    def _():
        pl.semaphore_wait(go.at[1], 1)

    far_first = [(2, 1), (1, 1), (3, 1), (2, 0), (1, 0), (3, 0), (0, 1)]
    others = [((n // 2 + dx) % (narrows // 2)) * 2 + (n + dl) % 2 for dx, dl in far_first]
    def send_patches(targets):
        for other in targets:
            sent(x_all.at[n], x_all.at[n], out_sem.at[0], gx.at[0], (w, other)).start()

    send_patches(others[:3])

    per = x.shape[0]
    other = rolled(x, 64)
    low = lax.broadcasted_iota(jnp.int32, x.shape, 1) < 64
    twice = jnp.concatenate([jnp.where(low, x, other), jnp.where(low, other, x)], axis=0).astype(BF16)
    squares = jnp.zeros((2 * per, LANES), F32)
    step = 512
    for k in range(width // step):
        piece = pl.ds(k * step, step)
        centre = dot(twice, wst[:, piece]) + (pb_v[:, piece] - bias_mean)
        centre = centre * centre
        for i in range(step // LANES):
            squares = squares + centre[:, i * LANES : (i + 1) * LANES]
    spread = jnp.sum(squares, axis=1, keepdims=True) * (1.0 / width)
    factor = lax.rsqrt(spread + 1e-06)
    lane2 = lax.broadcasted_iota(jnp.int32, (per, LANES), 1)
    chosen = jnp.where(lane2 < 3, factor[:per], factor[per:])
    hi = chosen.astype(BF16).astype(F32)
    mid = (chosen - hi).astype(BF16).astype(F32)
    chosen = jnp.where(lane2 % 3 == 0, hi, jnp.where(lane2 % 3 == 1, mid, chosen - hi - mid))
    placed = jnp.where(lane2 < 6, chosen, jnp.where(lane2 == 6, 1.0, 0.0))
    placed = jnp.concatenate([placed, jnp.zeros((LANES - per, LANES), F32)], axis=0)
    r_all[n] = jnp.transpose(placed)[:16].astype(BF16)
    for other in others:
        sent(r_all.at[n], r_all.at[n], out_sem.at[0], gx.at[1], (w, other)).start()
    send_patches(others[3:])

    @pl.when(jnp.logical_and(sums, chip_z == 0))
    def _():
        first_sums()

    def spread(p, c):
        mine = m_all.at[pl.ds(each * chip_y + half * p, half)]
        for y in range(highs):

            @pl.when(jnp.logical_or(y != chip_y, c != core))
            def _():
                sent(mine, mine, out_sem.at[0], g1.at[4], at(y, chip_z, c)).start()

    @pl.when(sums)
    def _():
        for p in range(2):
            landed(got2.at[p], g1.at[2 + p])
            total = own32[p]
            for i in range(1, DEPTHS):
                total = total + got2[p, i - 1].astype(F32)
            for k in range(half):
                plain = total[k]
                both = plain + pltpu.roll(plain, 14, 0)
                hi = both.astype(BF16).astype(F32)
                both = jnp.where(row16 < 2, hi, pltpu.roll(both - hi, 2, 0))
                tile = each * chip_y + half * p + k
                m_all[tile] = jnp.where(tile % 5 == 4, both, plain).astype(BF16)
            spread(p, CORES - 1)
        for p in range(2):
            spread(p, 0)

    landed(qb_v, in_sem.at[5])
    landed(ng_v, in_sem.at[6])
    e_out[0:3] = qb_v[...]
    e_out[3:5, :LANES] = ng_v[...]
    landed(x_all.at[pl.ds(0, narrows - 1)], gx.at[0])
    landed(r_all.at[pl.ds(0, narrows - 1)], gx.at[1])
    term = lax.broadcasted_iota(jnp.int32, (16, 3 * LANES), 0)
    place = lax.broadcasted_iota(jnp.int32, (16, 3 * LANES), 1)
    spot = place % LANES
    frame = jnp.where(place < LANES, spot // 64, place // LANES - 1)
    wanted = jnp.where(place < LANES, 0, jnp.where(spot < 3, 1, jnp.where(spot < 5, 2, 3)))
    taken = (wanted == 0) & (term // 3 == frame)
    taken = taken | ((wanted == 1) & (term == 3 * frame + spot % 2)) | ((wanted == 2) & (term == 6))
    spread_out = jnp.where(taken, 1.0, 0.0).astype(BF16)
    for src in range(narrows):
        table = lax.dot_general(
            r_all[src], spread_out, (((0,), (0,)), ((), ())), preferred_element_type=F32
        )[:per]
        value = x_all[src].astype(F32) * table[:, :LANES]
        hi = value.astype(BF16).astype(F32)
        lo = value - hi
        crossed = rolled(jnp.where(low, lo, hi), 64)
        values = [jnp.where(low, hi, crossed), jnp.where(low, crossed, lo)]
        for t in range(2):
            place = pl.ds((t * narrows + src) * per, per)
            x_out[place, :LANES] = values[t].astype(BF16)
            x_out[place, LANES:] = table[:, LANES * (t + 1) : LANES * (t + 2)].astype(BF16)
    @pl.when(sums)
    def _():
        landed(m_all.at[pl.ds(0, each * (highs - 1))], g1.at[4])

    @pl.when(jnp.logical_not(sums))
    def _():
        landed(m_all, g1.at[4])

    m_out[...] = m_all[...]
    always = (narrows - 1) * (lines(x_all) + lines(r_all)) // narrows
    spread_lines = (CORES * highs - 1) * lines(m_all) // highs
    for sides in (1, 2):
        for follows in (False, True):
            for adds in (False, True):
                gone = always + sides * edge + (main + sides * edge if follows else 0)
                gone += lines(got1, got2) + spread_lines if adds else lines(part)
                here_so = jnp.logical_and(beside == sides, has_next == follows)

                @pl.when(jnp.logical_and(here_so, sums == adds))
                def _():
                    landed_lines(gone, out_sem.at[0])


def back(x_ref, m_ref, e_ref, out, mm, stage, sems):
    tokens = x_ref.shape[0] // 2
    row16 = lax.broadcasted_iota(jnp.int32, (16, LANES), 0)
    mm[144:] = jnp.zeros((112, 768), BF16)
    for head in range(2):
        for j in range(3):
            cols = slice(256 * j + LANES * head, 256 * j + LANES * (head + 1))
            tile = 15 * head + 5 * j
            block = m_ref[tile : tile + 4].reshape(64, LANES)
            mm[:64, cols] = block
            mm[64:128, cols] = block
            extra = m_ref[tile + 4].astype(F32)
            constant = extra[1:2] + extra[3:4] + e_ref[j : j + 1, LANES * head : LANES * (head + 1)]
            high = constant.astype(BF16).astype(F32)
            rows = jnp.where(row16 < 2, extra[0:1], 0.0)
            rows = jnp.where(row16 == 2, extra[2:3], rows)
            rows = jnp.where(row16 == 3, high, rows)
            rows = jnp.where(row16 == 4, constant - high, rows)
            mm[128:144, cols] = rows.astype(BF16)
    half = tokens // 2
    for part in range(4):
        for j in range(3):
            place = pl.ds(part * half, half)
            product = dot(x_ref[place], mm[:, 256 * j : 256 * j + 256])
            for hd in range(2):
                cols = slice(LANES * hd, LANES * hd + LANES)
                y = product[:, cols]
                if j < 2:
                    mean = jnp.sum(y * y, axis=1, keepdims=True) * (1.0 / LANES)
                    y = y * lax.rsqrt(mean + 1e-06) * e_ref[3 + j : 4 + j, :LANES]
                stage[j, place, cols] = y.astype(BF16)
            copy = pltpu.make_async_copy(stage.at[j, place], out.at[j, place], sems.at[0])
            copy.start()
    pltpu.make_async_copy(stage, out, sems.at[0]).wait()


def local(wides, narrows, activations, conv_weight, patch_weight, patch_bias, shift, scale, qkv_weight, qkv_bias, norm_gains):
    rows, cols, channels = activations.shape[1:]
    width = patch_weight.shape[1]
    taps = jnp.transpose(conv_weight, (0, 1, 2, 4, 3)).reshape(-1, channels)
    qkv = jnp.transpose(qkv_weight, (1, 0, 2))
    highs = wides // (CORES * DEPTHS)
    half = -(-30 // (2 * highs))
    per = rows // 2 * cols // 2
    any_spec = pl.BlockSpec(memory_space=pltpu.HBM)
    vmem = pl.BlockSpec(memory_space=pltpu.VMEM)
    dma = pltpu.SemaphoreType.DMA
    edge = pltpu.VMEM((16, LANES), F32)
    x, m, e = pl.pallas_call(
        functools.partial(front, (wides, narrows, rows, width)),
        out_shape=[
            jax.ShapeDtypeStruct((2 * narrows * per, 2 * LANES), BF16),
            jax.ShapeDtypeStruct((highs * 2 * half, 16, LANES), BF16),
            jax.ShapeDtypeStruct((8, 256), F32),
        ],
        in_specs=[any_spec] * 9,
        out_specs=[vmem] * 3,
        scratch_shapes=[
            pltpu.VMEM((rows, 2, cols, channels), BF16),
            pltpu.VMEM(taps.shape, BF16),
            pltpu.VMEM(patch_weight.shape, BF16),
            pltpu.VMEM((1, width), F32),
            pltpu.VMEM((1, width), F32),
            pltpu.VMEM((1, width), F32),
            pltpu.VMEM((3, LANES, 256), BF16),
            pltpu.VMEM(qkv_bias.shape, F32),
            pltpu.VMEM(norm_gains.shape, F32),
            pltpu.VMEM((30, 16, LANES), F32),
            pltpu.VMEM((30, 16, LANES), F32),
            pltpu.VMEM((2, highs, half, 16, LANES), BF16),
            pltpu.VMEM((2, highs - 1, half, 16, LANES), BF16),
            pltpu.VMEM((2, half, 16, LANES), BF16),
            pltpu.VMEM((2, half, 16, LANES), F32),
            pltpu.VMEM((2, DEPTHS - 1, half, 16, LANES), BF16),
            pltpu.VMEM((highs * 2 * half, 16, LANES), BF16),
            pltpu.VMEM((rows, taps.shape[0], LANES), F32),
            pltpu.VMEM((rows + 2, 16, LANES), F32),
            pltpu.VMEM((rows + 2, 16, LANES), F32),
            edge,
            edge,
            pltpu.VMEM((rows, 16, LANES), F32),
            edge,
            edge,
            pltpu.VMEM((LANES, width), BF16),
            pltpu.VMEM((narrows, per, LANES), BF16),
            pltpu.VMEM((narrows, 16, LANES), BF16),
            dma((7,)),
            pltpu.SemaphoreType.REGULAR((2,)),
            dma((1,)),
            dma((1,)),
            dma((5,)),
            dma((2,)),
            dma((1,)),
        ],
        compiler_params=pltpu.CompilerParams(
            collective_id=0, has_side_effects=True, vmem_limit_bytes=40 * 1024 * 1024
        ),
        name="front",
    )(
        *(
            pltpu.with_memory_space_constraint(a, pltpu.HBM)
            for a in (
                activations,
                taps,
                patch_weight,
                patch_bias.reshape(1, -1),
                shift.reshape(1, -1),
                scale.reshape(1, -1),
                qkv,
                qkv_bias,
                norm_gains,
            )
        )
    )
    tokens = narrows * per
    return pl.pallas_call(
        back,
        out_shape=jax.ShapeDtypeStruct((3, 2 * tokens, 256), BF16),
        in_specs=[vmem] * 3,
        out_specs=any_spec,
        scratch_shapes=[
            pltpu.VMEM((2 * LANES, 768), BF16),
            pltpu.VMEM((3, 2 * tokens, 256), BF16),
            dma((1,)),
        ],
        compiler_params=pltpu.CompilerParams(vmem_limit_bytes=40 * 1024 * 1024),
        name="back",
    )(x, m, e)


def solution(mesh):
    placed = (
        P("wide", "narrow", None, None),
        P(),
        P(),
        P(),
        P(),
        P(),
        P("wide", None, "narrow"),
        P(None, "narrow"),
        P(),
    )
    return jax.shard_map(
        functools.partial(local, mesh.shape["wide"], mesh.shape["narrow"]),
        mesh=mesh,
        in_specs=placed,
        out_specs=P(None, "wide", "narrow"),
        check_vma=False,
    )
```

```python
import functools
import math

import jax
import jax.numpy as jnp
from jax import lax
from jax.experimental import pallas as pl
from jax.experimental.pallas import tpu as pltpu
from jax.sharding import PartitionSpec as P

MESH = pl.DeviceIdType.MESH
F32 = jnp.float32
BF16 = jnp.bfloat16
DEPTHS = 4
CORES = 2
LANES = 128


def rolled(x, by):
    return pltpu.roll(x, by % x.shape[1], 1)


def halves(x):
    high = x.astype(BF16)
    return high, (x - high.astype(F32)).astype(BF16)


def dot(a, b):
    return lax.dot_general(a, b, (((1,), (0,)), ((), ())), preferred_element_type=F32)


def dot_t(a, b):
    return lax.dot_general(a, b, (((1,), (1,)), ((), ())), preferred_element_type=F32)


def front(
    sizes,
    act, cw, pw, pb, sh, sc, qw, qb, ng,
    x_out, m_out, e_out,
    act_v, cw_v, pw_v, pb_v, sh_v, sc_v, qw_v, qb_v, ng_v,
    part, pair, share, got1, own, own32, got2, m_all, prod,
    a_v, b_v, at_v, ab_v, bm_v, bt_v, bb_v,
    wst, x_all, r_all,
    in_sem, go, out_sem, g0, g1, gx, gh_sem,
):
    wides, narrows, rows, width = sizes
    span = qw.shape[1]
    w = lax.axis_index("wide")
    n = lax.axis_index("narrow")
    pairs = rows // 2
    chips = wides // CORES
    core = w % CORES
    me = w // CORES
    partner = w + 1 - 2 * core
    sums = core == CORES - 1

    chip_y = me // DEPTHS
    chip_z = me % DEPTHS
    highs = chips // DEPTHS
    half = share.shape[2]
    each = 2 * half

    def at(y, z, c):
        return (y % highs * DEPTHS + z % DEPTHS) * CORES + c, n

    def core1(y, z):
        return at(y, z, CORES - 1)

    def landed(ref, sem):
        pltpu.make_async_copy(ref, ref, sem).wait()

    def lines(*refs):
        return sum(math.prod(ref.shape) * ref.dtype.itemsize for ref in refs) // (4 * LANES)

    def landed_lines(count, sem):
        planes = 4 if count % 4 == 0 and count // 4 <= prod.shape[1] else rows
        landed(prod.at[pl.ds(0, planes), pl.ds(0, count // planes)], sem)

    qw_part = qw_v.at[:, pl.ds(0, span), :]
    small = [(sc, sc_v), (sh, sh_v), (pb, pb_v), (qb, qb_v), (ng, ng_v)]
    pltpu.make_async_copy(pw, pw_v, in_sem.at[0]).start()
    for k, (src, dst) in enumerate(small[:3]):
        pltpu.make_async_copy(src, dst, in_sem.at[2 + k]).start()
    pltpu.make_async_copy(qw, qw_part, in_sem.at[0]).start()
    pltpu.make_async_copy(cw, cw_v, in_sem.at[1]).start()
    for t in range(2):
        pltpu.make_async_copy(act.at[t], act_v.at[:, t], in_sem.at[1]).start()
    for k, (src, dst) in enumerate(small[3:]):
        pltpu.make_async_copy(src, dst, in_sem.at[5 + k]).start()

    barrier = pltpu.get_barrier_semaphore()

    def greet(wide, narrow):
        pl.semaphore_signal(barrier, inc=1, device_id=(wide, narrow), device_id_type=MESH)

    has_next = w < wides - 1
    has_prev = w > 0
    up = n > 0
    down = n < narrows - 1
    for i in range(1, highs):
        greet(*core1(chip_y + i, chip_z))
    for other in range(narrows):

        @pl.when(jnp.logical_or(n < other, n == other + 1))
        def _():
            greet(w + CORES - 1 - core, other)

    greet(partner, n)

    @pl.when(sums)
    def _():
        for i in range(1, DEPTHS):
            greet(*core1(chip_y, chip_z + i))

        @pl.when(up)
        def _():
            greet(w, n - 1)

        @pl.when(down)
        def _():
            greet(w, n + 1)

    @pl.when(jnp.logical_and(jnp.logical_not(sums), has_prev))
    def _():
        greet(w - 1, n)

        @pl.when(up)
        def _():
            greet(w - 1, n - 1)

        @pl.when(down)
        def _():
            greet(w - 1, n + 1)

    across = jnp.where(up, 1, 0) + jnp.where(down, 1, 0)
    expected = CORES * (n + jnp.where(down, 1, 0)) + across + jnp.where(has_next, 1 + across, 0) + CORES * (highs - 1) + DEPTHS

    qw_v[:, span:, :] = jnp.zeros((3, qw_v.shape[1] - span, qw_v.shape[2]), BF16)
    landed_lines(lines(pw_v, qw_part), in_sem.at[0])
    for k in range(3):
        landed(small[k][1], in_sem.at[2 + k])
    weight = pw_v[...].astype(F32)
    means = jnp.sum(weight, axis=1, keepdims=True) * (1.0 / width)
    bias_mean = jnp.sum(pb_v[...], axis=1, keepdims=True) * (1.0 / width)
    begin = w * span
    base = pl.multiple_of(jnp.minimum(begin // LANES, width // LANES - 2) * LANES, LANES)
    window = pl.ds(base, 2 * LANES)
    gain = 1.0 + sc_v[:, window]
    main = (pw_v[:, window].astype(F32) - means) * gain
    extra_b = (pb_v[:, window] - bias_mean) * gain
    extra_s = sh_v[:, window]
    pad = jnp.zeros((14, 2 * LANES), F32)
    stacked = jnp.concatenate([main, extra_b, extra_s, pad], axis=0)
    shift_by = (2 * LANES - (begin - base)) % (2 * LANES)
    stacked = pltpu.roll(stacked, shift_by, 1)[:, :LANES]
    lane = lax.broadcasted_iota(jnp.int32, stacked.shape, 1)
    stacked = jnp.where(lane < span, stacked, 0.0)
    hi, lo = halves(stacked)
    for j in range(3):
        res = dot(hi, qw_v[j]) + dot(lo, qw_v[j])
        for head in range(2):
            part[15 * head + 5 * j : 15 * head + 5 * j + 5] = res[:, head * LANES : (head + 1) * LANES].reshape(5, 16, LANES)
    def sent(src, dst, ssem, gsem, to):
        return pltpu.make_async_remote_copy(
            src_ref=src, dst_ref=dst, send_sem=ssem, recv_sem=gsem, device_id=to, device_id_type=MESH
        )

    pair_copy = sent(part, pair, out_sem.at[0], g0.at[0], (partner, n))

    @pl.when(jnp.logical_not(sums))
    def _():
        pl.semaphore_wait(barrier, 1)
        pair_copy.start()

    landed_lines(lines(cw_v, act_v), in_sem.at[1])
    for k in range(pairs):
        raw = act_v[2 * k : 2 * k + 2].reshape(256, act.shape[3]).astype(F32)
        less = 0.5 * raw
        acted = (less + less * jnp.tanh(less)).astype(BF16)
        res = dot_t(cw_v[...], acted)
        prod[2 * k] = res[:, :LANES]
        prod[2 * k + 1] = res[:, LANES:]

    full = (16 * (rows + 2), LANES)
    col = lax.broadcasted_iota(jnp.int32, full, 1) % 64
    early = lax.broadcasted_iota(jnp.int32, full, 1) < 64
    taps = []
    for a in range(3):
        moved = []
        for c in range(3):
            planes = []
            for h in range(-1, rows + 1):
                total = None
                for b in range(3):
                    src = h + b - 1
                    if 0 <= src < rows:
                        g = (a * 3 + b) * 3 + c
                        piece = prod[src, 16 * g : 16 * g + 16, :]
                        total = piece if total is None else total + piece
                planes.append(total)
            moved.append(jnp.concatenate(planes, axis=0))
        left = jnp.where(col == 0, 0.0, rolled(moved[0], 1))
        right = jnp.where(col == 63, 0.0, rolled(moved[2], -1))
        taps.append(moved[1] + left + right)
    swapped = rolled(taps[1], 64)
    here = taps[2] + jnp.where(early, 0.0, swapped)
    ahead = taps[0] + jnp.where(early, swapped, 0.0)
    copies = jnp.where(early, taps[1] + taps[0], rolled(taps[0], 64))
    here = here + jnp.where(w == 0, copies, 0.0)
    a_v[...] = here.reshape(rows + 2, 16, LANES)
    b_v[...] = ahead.reshape(rows + 2, 16, LANES)


    @pl.when(sums)
    def _():
        pl.semaphore_wait(barrier, expected)
        pl.semaphore_signal(go.at[0], inc=1, device_id=(partner, n), device_id_type=MESH)
        for other in range(narrows - 2):

            @pl.when(other + 1 < n)
            def _():
                pl.semaphore_signal(go.at[1], inc=1, device_id=(w, other), device_id_type=MESH)

    @pl.when(jnp.logical_not(sums))
    def _():
        pl.semaphore_wait(go.at[0], 1)

    edges = [
        (b_v.at[0], bb_v, jnp.logical_and(has_next, up), jnp.logical_and(has_prev, down), (w + 1, n - 1)),
        (b_v.at[rows + 1], bt_v, jnp.logical_and(has_next, down), jnp.logical_and(has_prev, up), (w + 1, n + 1)),
        (b_v.at[pl.ds(1, rows)], bm_v, has_next, has_prev, (w + 1, n)),
        (a_v.at[0], ab_v, up, down, (w, n - 1)),
        (a_v.at[rows + 1], at_v, down, up, (w, n + 1)),
    ]
    edge_copies = []
    for k, (src, dst, gives, gets, to) in enumerate(edges):
        copy = sent(src, dst, out_sem.at[0], gh_sem.at[0], to)
        edge_copies.append(copy)

        @pl.when(gives)
        def _():
            copy.start()

        @pl.when(jnp.logical_not(gets))
        def _():
            dst[...] = jnp.zeros(dst.shape, F32)

    row16 = lax.broadcasted_iota(jnp.int32, (16, LANES), 0)

    @pl.when(sums)
    def _():
        pair_copy.wait_recv()
        for tile in range(30):
            total = part[tile] + pair[tile]
            if tile % 5 == 4:
                hi = total.astype(BF16).astype(F32)
                total = jnp.where(row16 < 2, hi, pltpu.roll(total - hi, 2, 0))
            share[tile % each // half, tile // each, tile % half] = total.astype(BF16)
        for tile in range(30, highs * each):
            share[tile % each // half, tile // each, tile % half] = jnp.zeros((16, LANES), BF16)
        for p in range(2):
            for i in range(1, highs):
                to = (chip_y + i) % highs
                sent(share.at[p, to], got1.at[p, i - 1], out_sem.at[0], g1.at[p], core1(to, chip_z)).start()

    hi, lo = halves(weight - means)
    wst[:64] = hi
    wst[64:] = lo

    def first_sums():
        for p in range(2):
            landed(got1.at[p], g1.at[p])
            total = share[p, chip_y].astype(F32)
            for i in range(1, highs):
                total = total + got1[p, i - 1].astype(F32)
            own32[p] = total
            own[p] = total.astype(BF16)
            for z in range(DEPTHS):

                @pl.when(z != chip_z)
                def _():
                    slot = lax.rem(z - chip_z + DEPTHS, DEPTHS) - 1
                    sent(own.at[p], got2.at[p, slot], out_sem.at[0], g1.at[2 + p], core1(chip_y, z)).start()

    @pl.when(jnp.logical_and(sums, chip_z > 0))
    def _():
        first_sums()

    edge = lines(a_v.at[0])
    main = lines(bm_v)
    beside = jnp.where(up, 1, 0) + jnp.where(down, 1, 0)
    for sides in (1, 2):

        @pl.when(jnp.logical_and(beside == sides, has_prev))
        def _():
            landed_lines(main + 2 * sides * edge, gh_sem.at[0])

        @pl.when(jnp.logical_and(beside == sides, jnp.logical_not(has_prev)))
        def _():
            landed_lines(sides * edge, gh_sem.at[0])

    lane1 = lax.broadcasted_iota(jnp.int32, (16, LANES), 1)
    pick = jnp.where(
        (lax.broadcasted_iota(jnp.int32, (32, LANES), 1) % 64) // 2
        == lax.broadcasted_iota(jnp.int32, (32, LANES), 0),
        1.0,
        0.0,
    ).astype(BF16)
    latents = []
    for h in range(rows):
        value = a_v[h + 1] + bm_v[h]
        if h == 0:
            value = value + (at_v[...] + bt_v[...])
        if h == rows - 1:
            value = value + (ab_v[...] + bb_v[...])
        latents.append(value)
    patches = []
    for p in range(pairs):
        blocks = []
        for t in range(2):
            for u in range(2):
                for v in range(2):
                    keep = jnp.logical_and(lane1 // 64 == t, lane1 % 2 == v)
                    blocks.append(jnp.where(keep, latents[2 * p + u], 0.0).astype(BF16))
        patches.append(dot_t(pick, jnp.concatenate(blocks, axis=0)))
    x = jnp.concatenate(patches, axis=0)
    x_all[n] = x.astype(BF16)

    @pl.when(sums)
    def _():

        @pl.when(n < narrows - 2)
        def _():
            pl.semaphore_wait(go.at[1], narrows - 2 - n)

        pl.semaphore_signal(go.at[1], inc=1, device_id=(partner, n), device_id_type=MESH)

    @pl.when(jnp.logical_not(sums))
    def _():
        pl.semaphore_wait(go.at[1], 1)

    far_first = [(2, 1), (1, 1), (3, 1), (2, 0), (1, 0), (3, 0), (0, 1)]
    others = [((n // 2 + dx) % (narrows // 2)) * 2 + (n + dl) % 2 for dx, dl in far_first]
    def send_patches(targets):
        for other in targets:
            sent(x_all.at[n], x_all.at[n], out_sem.at[0], gx.at[0], (w, other)).start()

    send_patches(others[:4])

    per = x.shape[0]
    other = rolled(x, 64)
    low = lax.broadcasted_iota(jnp.int32, x.shape, 1) < 64
    twice = jnp.concatenate([jnp.where(low, x, other), jnp.where(low, other, x)], axis=0).astype(BF16)
    squares = jnp.zeros((2 * per, LANES), F32)
    step = 512
    for k in range(width // step):
        piece = pl.ds(k * step, step)
        centre = dot(twice, wst[:, piece]) + (pb_v[:, piece] - bias_mean)
        centre = centre * centre
        for i in range(step // LANES):
            squares = squares + centre[:, i * LANES : (i + 1) * LANES]
    spread = jnp.sum(squares, axis=1, keepdims=True) * (1.0 / width)
    factor = lax.rsqrt(spread + 1e-06)
    lane2 = lax.broadcasted_iota(jnp.int32, (per, LANES), 1)
    chosen = jnp.where(lane2 < 3, factor[:per], factor[per:])
    hi = chosen.astype(BF16).astype(F32)
    mid = (chosen - hi).astype(BF16).astype(F32)
    chosen = jnp.where(lane2 % 3 == 0, hi, jnp.where(lane2 % 3 == 1, mid, chosen - hi - mid))
    placed = jnp.where(lane2 < 6, chosen, jnp.where(lane2 == 6, 1.0, 0.0))
    placed = jnp.concatenate([placed, jnp.zeros((LANES - per, LANES), F32)], axis=0)
    r_all[n] = jnp.transpose(placed)[:16].astype(BF16)
    for other in others:
        sent(r_all.at[n], r_all.at[n], out_sem.at[0], gx.at[1], (w, other)).start()
    send_patches(others[4:])

    @pl.when(jnp.logical_and(sums, chip_z == 0))
    def _():
        first_sums()

    def spread(p, c):
        mine = m_all.at[pl.ds(each * chip_y + half * p, half)]
        for y in range(highs):

            @pl.when(jnp.logical_or(y != chip_y, c != core))
            def _():
                sent(mine, mine, out_sem.at[0], g1.at[4], at(y, chip_z, c)).start()

    @pl.when(sums)
    def _():
        for p in range(2):
            landed(got2.at[p], g1.at[2 + p])
            total = own32[p]
            for i in range(1, DEPTHS):
                total = total + got2[p, i - 1].astype(F32)
            for k in range(half):
                plain = total[k]
                both = plain + pltpu.roll(plain, 14, 0)
                hi = both.astype(BF16).astype(F32)
                both = jnp.where(row16 < 2, hi, pltpu.roll(both - hi, 2, 0))
                tile = each * chip_y + half * p + k
                m_all[tile] = jnp.where(tile % 5 == 4, both, plain).astype(BF16)
            spread(p, CORES - 1)
        for p in range(2):
            spread(p, 0)

    landed(qb_v, in_sem.at[5])
    landed(ng_v, in_sem.at[6])
    e_out[0:3] = qb_v[...]
    e_out[3:5, :LANES] = ng_v[...]
    landed(x_all.at[pl.ds(0, narrows - 1)], gx.at[0])
    landed(r_all.at[pl.ds(0, narrows - 1)], gx.at[1])
    term = lax.broadcasted_iota(jnp.int32, (16, 3 * LANES), 0)
    place = lax.broadcasted_iota(jnp.int32, (16, 3 * LANES), 1)
    spot = place % LANES
    frame = jnp.where(place < LANES, spot // 64, place // LANES - 1)
    wanted = jnp.where(place < LANES, 0, jnp.where(spot < 3, 1, jnp.where(spot < 5, 2, 3)))
    taken = (wanted == 0) & (term // 3 == frame)
    taken = taken | ((wanted == 1) & (term == 3 * frame + spot % 2)) | ((wanted == 2) & (term == 6))
    spread_out = jnp.where(taken, 1.0, 0.0).astype(BF16)
    for src in range(narrows):
        table = lax.dot_general(
            r_all[src], spread_out, (((0,), (0,)), ((), ())), preferred_element_type=F32
        )[:per]
        value = x_all[src].astype(F32) * table[:, :LANES]
        hi = value.astype(BF16).astype(F32)
        lo = value - hi
        crossed = rolled(jnp.where(low, lo, hi), 64)
        values = [jnp.where(low, hi, crossed), jnp.where(low, crossed, lo)]
        for t in range(2):
            place = pl.ds((t * narrows + src) * per, per)
            x_out[place, :LANES] = values[t].astype(BF16)
            x_out[place, LANES:] = table[:, LANES * (t + 1) : LANES * (t + 2)].astype(BF16)
    @pl.when(sums)
    def _():
        landed(m_all.at[pl.ds(0, each * (highs - 1))], g1.at[4])

    @pl.when(jnp.logical_not(sums))
    def _():
        landed(m_all, g1.at[4])

    m_out[...] = m_all[...]
    always = (narrows - 1) * (lines(x_all) + lines(r_all)) // narrows
    spread_lines = (CORES * highs - 1) * lines(m_all) // highs
    for sides in (1, 2):
        for follows in (False, True):
            for adds in (False, True):
                gone = always + sides * edge + (main + sides * edge if follows else 0)
                gone += lines(got1, got2) + spread_lines if adds else lines(part)
                here_so = jnp.logical_and(beside == sides, has_next == follows)

                @pl.when(jnp.logical_and(here_so, sums == adds))
                def _():
                    landed_lines(gone, out_sem.at[0])


def back(x_ref, m_ref, e_ref, out, mm, stage, sems):
    tokens = x_ref.shape[0] // 2
    row16 = lax.broadcasted_iota(jnp.int32, (16, LANES), 0)
    mm[144:] = jnp.zeros((112, 768), BF16)
    for head in range(2):
        for j in range(3):
            cols = slice(256 * j + LANES * head, 256 * j + LANES * (head + 1))
            tile = 15 * head + 5 * j
            block = m_ref[tile : tile + 4].reshape(64, LANES)
            mm[:64, cols] = block
            mm[64:128, cols] = block
            extra = m_ref[tile + 4].astype(F32)
            constant = extra[1:2] + extra[3:4] + e_ref[j : j + 1, LANES * head : LANES * (head + 1)]
            high = constant.astype(BF16).astype(F32)
            rows = jnp.where(row16 < 2, extra[0:1], 0.0)
            rows = jnp.where(row16 == 2, extra[2:3], rows)
            rows = jnp.where(row16 == 3, high, rows)
            rows = jnp.where(row16 == 4, constant - high, rows)
            mm[128:144, cols] = rows.astype(BF16)
    half = tokens // 2
    for part in range(4):
        for j in range(3):
            place = pl.ds(part * half, half)
            product = dot(x_ref[place], mm[:, 256 * j : 256 * j + 256])
            for hd in range(2):
                cols = slice(LANES * hd, LANES * hd + LANES)
                y = product[:, cols]
                if j < 2:
                    mean = jnp.sum(y * y, axis=1, keepdims=True) * (1.0 / LANES)
                    y = y * lax.rsqrt(mean + 1e-06) * e_ref[3 + j : 4 + j, :LANES]
                stage[j, place, cols] = y.astype(BF16)
            copy = pltpu.make_async_copy(stage.at[j, place], out.at[j, place], sems.at[0])
            copy.start()
    pltpu.make_async_copy(stage, out, sems.at[0]).wait()


def local(wides, narrows, activations, conv_weight, patch_weight, patch_bias, shift, scale, qkv_weight, qkv_bias, norm_gains):
    rows, cols, channels = activations.shape[1:]
    width = patch_weight.shape[1]
    taps = jnp.transpose(conv_weight, (0, 1, 2, 4, 3)).reshape(-1, channels)
    qkv = jnp.transpose(qkv_weight, (1, 0, 2))
    highs = wides // (CORES * DEPTHS)
    half = -(-30 // (2 * highs))
    per = rows // 2 * cols // 2
    any_spec = pl.BlockSpec(memory_space=pltpu.HBM)
    vmem = pl.BlockSpec(memory_space=pltpu.VMEM)
    dma = pltpu.SemaphoreType.DMA
    edge = pltpu.VMEM((16, LANES), F32)
    x, m, e = pl.pallas_call(
        functools.partial(front, (wides, narrows, rows, width)),
        out_shape=[
            jax.ShapeDtypeStruct((2 * narrows * per, 2 * LANES), BF16),
            jax.ShapeDtypeStruct((highs * 2 * half, 16, LANES), BF16),
            jax.ShapeDtypeStruct((8, 256), F32),
        ],
        in_specs=[any_spec] * 9,
        out_specs=[vmem] * 3,
        scratch_shapes=[
            pltpu.VMEM((rows, 2, cols, channels), BF16),
            pltpu.VMEM(taps.shape, BF16),
            pltpu.VMEM(patch_weight.shape, BF16),
            pltpu.VMEM((1, width), F32),
            pltpu.VMEM((1, width), F32),
            pltpu.VMEM((1, width), F32),
            pltpu.VMEM((3, LANES, 256), BF16),
            pltpu.VMEM(qkv_bias.shape, F32),
            pltpu.VMEM(norm_gains.shape, F32),
            pltpu.VMEM((30, 16, LANES), F32),
            pltpu.VMEM((30, 16, LANES), F32),
            pltpu.VMEM((2, highs, half, 16, LANES), BF16),
            pltpu.VMEM((2, highs - 1, half, 16, LANES), BF16),
            pltpu.VMEM((2, half, 16, LANES), BF16),
            pltpu.VMEM((2, half, 16, LANES), F32),
            pltpu.VMEM((2, DEPTHS - 1, half, 16, LANES), BF16),
            pltpu.VMEM((highs * 2 * half, 16, LANES), BF16),
            pltpu.VMEM((rows, taps.shape[0], LANES), F32),
            pltpu.VMEM((rows + 2, 16, LANES), F32),
            pltpu.VMEM((rows + 2, 16, LANES), F32),
            edge,
            edge,
            pltpu.VMEM((rows, 16, LANES), F32),
            edge,
            edge,
            pltpu.VMEM((LANES, width), BF16),
            pltpu.VMEM((narrows, per, LANES), BF16),
            pltpu.VMEM((narrows, 16, LANES), BF16),
            dma((7,)),
            pltpu.SemaphoreType.REGULAR((2,)),
            dma((1,)),
            dma((1,)),
            dma((5,)),
            dma((2,)),
            dma((1,)),
        ],
        compiler_params=pltpu.CompilerParams(
            collective_id=0, has_side_effects=True, vmem_limit_bytes=40 * 1024 * 1024
        ),
        name="front",
    )(
        *(
            pltpu.with_memory_space_constraint(a, pltpu.HBM)
            for a in (
                activations,
                taps,
                patch_weight,
                patch_bias.reshape(1, -1),
                shift.reshape(1, -1),
                scale.reshape(1, -1),
                qkv,
                qkv_bias,
                norm_gains,
            )
        )
    )
    tokens = narrows * per
    return pl.pallas_call(
        back,
        out_shape=jax.ShapeDtypeStruct((3, 2 * tokens, 256), BF16),
        in_specs=[vmem] * 3,
        out_specs=any_spec,
        scratch_shapes=[
            pltpu.VMEM((2 * LANES, 768), BF16),
            pltpu.VMEM((3, 2 * tokens, 256), BF16),
            dma((1,)),
        ],
        compiler_params=pltpu.CompilerParams(vmem_limit_bytes=40 * 1024 * 1024),
        name="back",
    )(x, m, e)


def solution(mesh):
    placed = (
        P("wide", "narrow", None, None),
        P(),
        P(),
        P(),
        P(),
        P(),
        P("wide", None, "narrow"),
        P(None, "narrow"),
        P(),
    )
    return jax.shard_map(
        functools.partial(local, mesh.shape["wide"], mesh.shape["narrow"]),
        mesh=mesh,
        in_specs=placed,
        out_specs=P(None, "wide", "narrow"),
        check_vma=False,
    )
```

```python
import functools
import math

import jax
import jax.numpy as jnp
from jax import lax
from jax.experimental import pallas as pl
from jax.experimental.pallas import tpu as pltpu
from jax.sharding import PartitionSpec as P

MESH = pl.DeviceIdType.MESH
F32 = jnp.float32
BF16 = jnp.bfloat16
DEPTHS = 4
CORES = 2
LANES = 128


def rolled(x, by):
    return pltpu.roll(x, by % x.shape[1], 1)


def halves(x):
    high = x.astype(BF16)
    return high, (x - high.astype(F32)).astype(BF16)


def dot(a, b):
    return lax.dot_general(a, b, (((1,), (0,)), ((), ())), preferred_element_type=F32)


def dot_t(a, b):
    return lax.dot_general(a, b, (((1,), (1,)), ((), ())), preferred_element_type=F32)


def front(
    sizes,
    act, cw, pw, pb, sh, sc, qw, qb, ng,
    x_out, m_out, e_out,
    act_v, cw_v, pw_v, pb_v, sh_v, sc_v, qw_v, qb_v, ng_v,
    part, pair, share, got1, own, own32, got2, m_all, prod,
    a_v, b_v, at_v, ab_v, bm_v, bt_v, bb_v,
    wst, x_all, r_all,
    in_sem, go, out_sem, g0, g1, gx, gh_sem,
):
    wides, narrows, rows, width = sizes
    span = qw.shape[1]
    w = lax.axis_index("wide")
    n = lax.axis_index("narrow")
    pairs = rows // 2
    chips = wides // CORES
    core = w % CORES
    me = w // CORES
    partner = w + 1 - 2 * core
    sums = core == CORES - 1

    chip_y = me // DEPTHS
    chip_z = me % DEPTHS
    highs = chips // DEPTHS
    half = share.shape[2]
    each = 2 * half

    def at(y, z, c):
        return (y % highs * DEPTHS + z % DEPTHS) * CORES + c, n

    def core1(y, z):
        return at(y, z, CORES - 1)

    def landed(ref, sem):
        pltpu.make_async_copy(ref, ref, sem).wait()

    def lines(*refs):
        return sum(math.prod(ref.shape) * ref.dtype.itemsize for ref in refs) // (4 * LANES)

    def landed_lines(count, sem):
        planes = 4 if count % 4 == 0 and count // 4 <= prod.shape[1] else rows
        landed(prod.at[pl.ds(0, planes), pl.ds(0, count // planes)], sem)

    qw_part = qw_v.at[:, pl.ds(0, span), :]
    small = [(sc, sc_v), (sh, sh_v), (pb, pb_v), (qb, qb_v), (ng, ng_v)]
    pltpu.make_async_copy(pw, pw_v, in_sem.at[0]).start()
    for k, (src, dst) in enumerate(small[:3]):
        pltpu.make_async_copy(src, dst, in_sem.at[2 + k]).start()
    pltpu.make_async_copy(qw, qw_part, in_sem.at[0]).start()
    pltpu.make_async_copy(cw, cw_v, in_sem.at[1]).start()
    for t in range(2):
        pltpu.make_async_copy(act.at[t], act_v.at[:, t], in_sem.at[1]).start()
    for k, (src, dst) in enumerate(small[3:]):
        pltpu.make_async_copy(src, dst, in_sem.at[5 + k]).start()

    barrier = pltpu.get_barrier_semaphore()

    def greet(wide, narrow):
        pl.semaphore_signal(barrier, inc=1, device_id=(wide, narrow), device_id_type=MESH)

    has_next = w < wides - 1
    has_prev = w > 0
    up = n > 0
    down = n < narrows - 1
    for i in range(1, highs):
        greet(*core1(chip_y + i, chip_z))
    for other in range(narrows):

        @pl.when(jnp.logical_or(n < other, n == other + 1))
        def _():
            greet(w + CORES - 1 - core, other)

    greet(partner, n)

    @pl.when(sums)
    def _():
        for i in range(1, DEPTHS):
            greet(*core1(chip_y, chip_z + i))

        @pl.when(up)
        def _():
            greet(w, n - 1)

        @pl.when(down)
        def _():
            greet(w, n + 1)

    @pl.when(jnp.logical_and(jnp.logical_not(sums), has_prev))
    def _():
        greet(w - 1, n)

        @pl.when(up)
        def _():
            greet(w - 1, n - 1)

        @pl.when(down)
        def _():
            greet(w - 1, n + 1)

    across = jnp.where(up, 1, 0) + jnp.where(down, 1, 0)
    expected = CORES * (n + jnp.where(down, 1, 0)) + across + jnp.where(has_next, 1 + across, 0) + CORES * (highs - 1) + DEPTHS

    qw_v[:, span:, :] = jnp.zeros((3, qw_v.shape[1] - span, qw_v.shape[2]), BF16)
    landed_lines(lines(pw_v, qw_part), in_sem.at[0])
    for k in range(3):
        landed(small[k][1], in_sem.at[2 + k])
    weight = pw_v[...].astype(F32)
    means = jnp.sum(weight, axis=1, keepdims=True) * (1.0 / width)
    bias_mean = jnp.sum(pb_v[...], axis=1, keepdims=True) * (1.0 / width)
    begin = w * span
    base = pl.multiple_of(jnp.minimum(begin // LANES, width // LANES - 2) * LANES, LANES)
    window = pl.ds(base, 2 * LANES)
    gain = 1.0 + sc_v[:, window]
    main = (pw_v[:, window].astype(F32) - means) * gain
    extra_b = (pb_v[:, window] - bias_mean) * gain
    extra_s = sh_v[:, window]
    pad = jnp.zeros((14, 2 * LANES), F32)
    stacked = jnp.concatenate([main, extra_b, extra_s, pad], axis=0)
    shift_by = (2 * LANES - (begin - base)) % (2 * LANES)
    stacked = pltpu.roll(stacked, shift_by, 1)[:, :LANES]
    lane = lax.broadcasted_iota(jnp.int32, stacked.shape, 1)
    stacked = jnp.where(lane < span, stacked, 0.0)
    hi, lo = halves(stacked)
    for j in range(3):
        res = dot(hi, qw_v[j]) + dot(lo, qw_v[j])
        for head in range(2):
            part[15 * head + 5 * j : 15 * head + 5 * j + 5] = res[:, head * LANES : (head + 1) * LANES].reshape(5, 16, LANES)
    def sent(src, dst, ssem, gsem, to):
        return pltpu.make_async_remote_copy(
            src_ref=src, dst_ref=dst, send_sem=ssem, recv_sem=gsem, device_id=to, device_id_type=MESH
        )

    pair_copy = sent(part, pair, out_sem.at[0], g0.at[0], (partner, n))

    @pl.when(jnp.logical_not(sums))
    def _():
        pl.semaphore_wait(barrier, 1)
        pair_copy.start()

    landed_lines(lines(cw_v, act_v), in_sem.at[1])
    for k in range(pairs):
        raw = act_v[2 * k : 2 * k + 2].reshape(256, act.shape[3]).astype(F32)
        less = 0.5 * raw
        acted = (less + less * jnp.tanh(less)).astype(BF16)
        res = dot_t(cw_v[...], acted)
        prod[2 * k] = res[:, :LANES]
        prod[2 * k + 1] = res[:, LANES:]

    full = (16 * (rows + 2), LANES)
    col = lax.broadcasted_iota(jnp.int32, full, 1) % 64
    early = lax.broadcasted_iota(jnp.int32, full, 1) < 64
    taps = []
    for a in range(3):
        moved = []
        for c in range(3):
            planes = []
            for h in range(-1, rows + 1):
                total = None
                for b in range(3):
                    src = h + b - 1
                    if 0 <= src < rows:
                        g = (a * 3 + b) * 3 + c
                        piece = prod[src, 16 * g : 16 * g + 16, :]
                        total = piece if total is None else total + piece
                planes.append(total)
            moved.append(jnp.concatenate(planes, axis=0))
        left = jnp.where(col == 0, 0.0, rolled(moved[0], 1))
        right = jnp.where(col == 63, 0.0, rolled(moved[2], -1))
        taps.append(moved[1] + left + right)
    swapped = rolled(taps[1], 64)
    here = taps[2] + jnp.where(early, 0.0, swapped)
    ahead = taps[0] + jnp.where(early, swapped, 0.0)
    copies = jnp.where(early, taps[1] + taps[0], rolled(taps[0], 64))
    here = here + jnp.where(w == 0, copies, 0.0)
    a_v[...] = here.reshape(rows + 2, 16, LANES)
    b_v[...] = ahead.reshape(rows + 2, 16, LANES)


    @pl.when(sums)
    def _():
        pl.semaphore_wait(barrier, expected)
        pl.semaphore_signal(go.at[0], inc=1, device_id=(partner, n), device_id_type=MESH)
        for other in range(narrows - 2):

            @pl.when(other + 1 < n)
            def _():
                pl.semaphore_signal(go.at[1], inc=1, device_id=(w, other), device_id_type=MESH)

    @pl.when(jnp.logical_not(sums))
    def _():
        pl.semaphore_wait(go.at[0], 1)

    edges = [
        (b_v.at[0], bb_v, jnp.logical_and(has_next, up), jnp.logical_and(has_prev, down), (w + 1, n - 1)),
        (b_v.at[rows + 1], bt_v, jnp.logical_and(has_next, down), jnp.logical_and(has_prev, up), (w + 1, n + 1)),
        (b_v.at[pl.ds(1, rows)], bm_v, has_next, has_prev, (w + 1, n)),
        (a_v.at[0], ab_v, up, down, (w, n - 1)),
        (a_v.at[rows + 1], at_v, down, up, (w, n + 1)),
    ]
    edge_copies = []
    for k, (src, dst, gives, gets, to) in enumerate(edges):
        copy = sent(src, dst, out_sem.at[0], gh_sem.at[0], to)
        edge_copies.append(copy)

        @pl.when(gives)
        def _():
            copy.start()

        @pl.when(jnp.logical_not(gets))
        def _():
            dst[...] = jnp.zeros(dst.shape, F32)

    row16 = lax.broadcasted_iota(jnp.int32, (16, LANES), 0)

    @pl.when(sums)
    def _():
        pair_copy.wait_recv()
        for tile in range(30):
            total = part[tile] + pair[tile]
            if tile % 5 == 4:
                hi = total.astype(BF16).astype(F32)
                total = jnp.where(row16 < 2, hi, pltpu.roll(total - hi, 2, 0))
            share[tile % each // half, tile // each, tile % half] = total.astype(BF16)
        for tile in range(30, highs * each):
            share[tile % each // half, tile // each, tile % half] = jnp.zeros((16, LANES), BF16)
        for p in range(2):
            for i in range(1, highs):
                to = (chip_y + i) % highs
                sent(share.at[p, to], got1.at[p, i - 1], out_sem.at[0], g1.at[p], core1(to, chip_z)).start()

    hi, lo = halves(weight - means)
    wst[:64] = hi
    wst[64:] = lo

    def send_own(p, z):
        @pl.when(z != chip_z)
        def _():
            slot = lax.rem(z - chip_z + DEPTHS, DEPTHS) - 1
            sent(own.at[p], got2.at[p, slot], out_sem.at[0], g1.at[2 + p], core1(chip_y, z)).start()

    def first_sums():
        for p in range(2):
            landed(got1.at[p], g1.at[p])
            total = share[p, chip_y].astype(F32)
            for i in range(1, highs):
                total = total + got1[p, i - 1].astype(F32)
            own32[p] = total
            own[p] = total.astype(BF16)
            send_own(p, 0)
        for z in range(1, DEPTHS):
            for p in range(2):
                send_own(p, z)

    @pl.when(jnp.logical_and(sums, chip_z > 0))
    def _():
        first_sums()

    edge = lines(a_v.at[0])
    main = lines(bm_v)
    beside = jnp.where(up, 1, 0) + jnp.where(down, 1, 0)
    for sides in (1, 2):

        @pl.when(jnp.logical_and(beside == sides, has_prev))
        def _():
            landed_lines(main + 2 * sides * edge, gh_sem.at[0])

        @pl.when(jnp.logical_and(beside == sides, jnp.logical_not(has_prev)))
        def _():
            landed_lines(sides * edge, gh_sem.at[0])

    lane1 = lax.broadcasted_iota(jnp.int32, (16, LANES), 1)
    pick = jnp.where(
        (lax.broadcasted_iota(jnp.int32, (32, LANES), 1) % 64) // 2
        == lax.broadcasted_iota(jnp.int32, (32, LANES), 0),
        1.0,
        0.0,
    ).astype(BF16)
    latents = []
    for h in range(rows):
        value = a_v[h + 1] + bm_v[h]
        if h == 0:
            value = value + (at_v[...] + bt_v[...])
        if h == rows - 1:
            value = value + (ab_v[...] + bb_v[...])
        latents.append(value)
    patches = []
    for p in range(pairs):
        blocks = []
        for t in range(2):
            for u in range(2):
                for v in range(2):
                    keep = jnp.logical_and(lane1 // 64 == t, lane1 % 2 == v)
                    blocks.append(jnp.where(keep, latents[2 * p + u], 0.0).astype(BF16))
        patches.append(dot_t(pick, jnp.concatenate(blocks, axis=0)))
    x = jnp.concatenate(patches, axis=0)
    x_all[n] = x.astype(BF16)

    @pl.when(sums)
    def _():

        @pl.when(n < narrows - 2)
        def _():
            pl.semaphore_wait(go.at[1], narrows - 2 - n)

        pl.semaphore_signal(go.at[1], inc=1, device_id=(partner, n), device_id_type=MESH)

    @pl.when(jnp.logical_not(sums))
    def _():
        pl.semaphore_wait(go.at[1], 1)

    far_first = [(2, 1), (1, 1), (3, 1), (2, 0), (1, 0), (3, 0), (0, 1)]
    others = [((n // 2 + dx) % (narrows // 2)) * 2 + (n + dl) % 2 for dx, dl in far_first]
    def send_patches(targets):
        for other in targets:
            sent(x_all.at[n], x_all.at[n], out_sem.at[0], gx.at[0], (w, other)).start()

    send_patches(others[:4])

    per = x.shape[0]
    other = rolled(x, 64)
    low = lax.broadcasted_iota(jnp.int32, x.shape, 1) < 64
    twice = jnp.concatenate([jnp.where(low, x, other), jnp.where(low, other, x)], axis=0).astype(BF16)
    squares = jnp.zeros((2 * per, LANES), F32)
    step = 512
    for k in range(width // step):
        piece = pl.ds(k * step, step)
        centre = dot(twice, wst[:, piece]) + (pb_v[:, piece] - bias_mean)
        centre = centre * centre
        for i in range(step // LANES):
            squares = squares + centre[:, i * LANES : (i + 1) * LANES]
    spread = jnp.sum(squares, axis=1, keepdims=True) * (1.0 / width)
    factor = lax.rsqrt(spread + 1e-06)
    lane2 = lax.broadcasted_iota(jnp.int32, (per, LANES), 1)
    chosen = jnp.where(lane2 < 3, factor[:per], factor[per:])
    hi = chosen.astype(BF16).astype(F32)
    mid = (chosen - hi).astype(BF16).astype(F32)
    chosen = jnp.where(lane2 % 3 == 0, hi, jnp.where(lane2 % 3 == 1, mid, chosen - hi - mid))
    placed = jnp.where(lane2 < 6, chosen, jnp.where(lane2 == 6, 1.0, 0.0))
    placed = jnp.concatenate([placed, jnp.zeros((LANES - per, LANES), F32)], axis=0)
    r_all[n] = jnp.transpose(placed)[:16].astype(BF16)
    for other in others:
        sent(r_all.at[n], r_all.at[n], out_sem.at[0], gx.at[1], (w, other)).start()
    send_patches(others[4:])

    @pl.when(jnp.logical_and(sums, chip_z == 0))
    def _():
        first_sums()

    def spread(p, c):
        mine = m_all.at[pl.ds(each * chip_y + half * p, half)]
        for y in range(highs):

            @pl.when(jnp.logical_or(y != chip_y, c != core))
            def _():
                sent(mine, mine, out_sem.at[0], g1.at[4], at(y, chip_z, c)).start()

    @pl.when(sums)
    def _():
        for p in range(2):
            landed(got2.at[p], g1.at[2 + p])
            total = own32[p]
            for i in range(1, DEPTHS):
                total = total + got2[p, i - 1].astype(F32)
            for k in range(half):
                plain = total[k]
                both = plain + pltpu.roll(plain, 14, 0)
                hi = both.astype(BF16).astype(F32)
                both = jnp.where(row16 < 2, hi, pltpu.roll(both - hi, 2, 0))
                tile = each * chip_y + half * p + k
                m_all[tile] = jnp.where(tile % 5 == 4, both, plain).astype(BF16)
            spread(p, CORES - 1)
        for p in range(2):
            spread(p, 0)

    landed(qb_v, in_sem.at[5])
    landed(ng_v, in_sem.at[6])
    e_out[0:3] = qb_v[...]
    e_out[3:5, :LANES] = ng_v[...]
    landed(x_all.at[pl.ds(0, narrows - 1)], gx.at[0])
    landed(r_all.at[pl.ds(0, narrows - 1)], gx.at[1])
    term = lax.broadcasted_iota(jnp.int32, (16, 3 * LANES), 0)
    place = lax.broadcasted_iota(jnp.int32, (16, 3 * LANES), 1)
    spot = place % LANES
    frame = jnp.where(place < LANES, spot // 64, place // LANES - 1)
    wanted = jnp.where(place < LANES, 0, jnp.where(spot < 3, 1, jnp.where(spot < 5, 2, 3)))
    taken = (wanted == 0) & (term // 3 == frame)
    taken = taken | ((wanted == 1) & (term == 3 * frame + spot % 2)) | ((wanted == 2) & (term == 6))
    spread_out = jnp.where(taken, 1.0, 0.0).astype(BF16)
    for src in range(narrows):
        table = lax.dot_general(
            r_all[src], spread_out, (((0,), (0,)), ((), ())), preferred_element_type=F32
        )[:per]
        value = x_all[src].astype(F32) * table[:, :LANES]
        hi = value.astype(BF16).astype(F32)
        lo = value - hi
        crossed = rolled(jnp.where(low, lo, hi), 64)
        values = [jnp.where(low, hi, crossed), jnp.where(low, crossed, lo)]
        for t in range(2):
            place = pl.ds((t * narrows + src) * per, per)
            x_out[place, :LANES] = values[t].astype(BF16)
            x_out[place, LANES:] = table[:, LANES * (t + 1) : LANES * (t + 2)].astype(BF16)
    @pl.when(sums)
    def _():
        landed(m_all.at[pl.ds(0, each * (highs - 1))], g1.at[4])

    @pl.when(jnp.logical_not(sums))
    def _():
        landed(m_all, g1.at[4])

    m_out[...] = m_all[...]
    always = (narrows - 1) * (lines(x_all) + lines(r_all)) // narrows
    spread_lines = (CORES * highs - 1) * lines(m_all) // highs
    for sides in (1, 2):
        for follows in (False, True):
            for adds in (False, True):
                gone = always + sides * edge + (main + sides * edge if follows else 0)
                gone += lines(got1, got2) + spread_lines if adds else lines(part)
                here_so = jnp.logical_and(beside == sides, has_next == follows)

                @pl.when(jnp.logical_and(here_so, sums == adds))
                def _():
                    landed_lines(gone, out_sem.at[0])


def back(x_ref, m_ref, e_ref, out, mm, stage, sems):
    tokens = x_ref.shape[0] // 2
    row16 = lax.broadcasted_iota(jnp.int32, (16, LANES), 0)
    mm[144:] = jnp.zeros((112, 768), BF16)
    for head in range(2):
        for j in range(3):
            cols = slice(256 * j + LANES * head, 256 * j + LANES * (head + 1))
            tile = 15 * head + 5 * j
            block = m_ref[tile : tile + 4].reshape(64, LANES)
            mm[:64, cols] = block
            mm[64:128, cols] = block
            extra = m_ref[tile + 4].astype(F32)
            constant = extra[1:2] + extra[3:4] + e_ref[j : j + 1, LANES * head : LANES * (head + 1)]
            high = constant.astype(BF16).astype(F32)
            rows = jnp.where(row16 < 2, extra[0:1], 0.0)
            rows = jnp.where(row16 == 2, extra[2:3], rows)
            rows = jnp.where(row16 == 3, high, rows)
            rows = jnp.where(row16 == 4, constant - high, rows)
            mm[128:144, cols] = rows.astype(BF16)
    half = tokens // 2
    for part in range(4):
        for j in range(3):
            place = pl.ds(part * half, half)
            product = dot(x_ref[place], mm[:, 256 * j : 256 * j + 256])
            for hd in range(2):
                cols = slice(LANES * hd, LANES * hd + LANES)
                y = product[:, cols]
                if j < 2:
                    mean = jnp.sum(y * y, axis=1, keepdims=True) * (1.0 / LANES)
                    y = y * lax.rsqrt(mean + 1e-06) * e_ref[3 + j : 4 + j, :LANES]
                stage[j, place, cols] = y.astype(BF16)
            copy = pltpu.make_async_copy(stage.at[j, place], out.at[j, place], sems.at[0])
            copy.start()
    pltpu.make_async_copy(stage, out, sems.at[0]).wait()


def local(wides, narrows, activations, conv_weight, patch_weight, patch_bias, shift, scale, qkv_weight, qkv_bias, norm_gains):
    rows, cols, channels = activations.shape[1:]
    width = patch_weight.shape[1]
    taps = jnp.transpose(conv_weight, (0, 1, 2, 4, 3)).reshape(-1, channels)
    qkv = jnp.transpose(qkv_weight, (1, 0, 2))
    highs = wides // (CORES * DEPTHS)
    half = -(-30 // (2 * highs))
    per = rows // 2 * cols // 2
    any_spec = pl.BlockSpec(memory_space=pltpu.HBM)
    vmem = pl.BlockSpec(memory_space=pltpu.VMEM)
    dma = pltpu.SemaphoreType.DMA
    edge = pltpu.VMEM((16, LANES), F32)
    x, m, e = pl.pallas_call(
        functools.partial(front, (wides, narrows, rows, width)),
        out_shape=[
            jax.ShapeDtypeStruct((2 * narrows * per, 2 * LANES), BF16),
            jax.ShapeDtypeStruct((highs * 2 * half, 16, LANES), BF16),
            jax.ShapeDtypeStruct((8, 256), F32),
        ],
        in_specs=[any_spec] * 9,
        out_specs=[vmem] * 3,
        scratch_shapes=[
            pltpu.VMEM((rows, 2, cols, channels), BF16),
            pltpu.VMEM(taps.shape, BF16),
            pltpu.VMEM(patch_weight.shape, BF16),
            pltpu.VMEM((1, width), F32),
            pltpu.VMEM((1, width), F32),
            pltpu.VMEM((1, width), F32),
            pltpu.VMEM((3, LANES, 256), BF16),
            pltpu.VMEM(qkv_bias.shape, F32),
            pltpu.VMEM(norm_gains.shape, F32),
            pltpu.VMEM((30, 16, LANES), F32),
            pltpu.VMEM((30, 16, LANES), F32),
            pltpu.VMEM((2, highs, half, 16, LANES), BF16),
            pltpu.VMEM((2, highs - 1, half, 16, LANES), BF16),
            pltpu.VMEM((2, half, 16, LANES), BF16),
            pltpu.VMEM((2, half, 16, LANES), F32),
            pltpu.VMEM((2, DEPTHS - 1, half, 16, LANES), BF16),
            pltpu.VMEM((highs * 2 * half, 16, LANES), BF16),
            pltpu.VMEM((rows, taps.shape[0], LANES), F32),
            pltpu.VMEM((rows + 2, 16, LANES), F32),
            pltpu.VMEM((rows + 2, 16, LANES), F32),
            edge,
            edge,
            pltpu.VMEM((rows, 16, LANES), F32),
            edge,
            edge,
            pltpu.VMEM((LANES, width), BF16),
            pltpu.VMEM((narrows, per, LANES), BF16),
            pltpu.VMEM((narrows, 16, LANES), BF16),
            dma((7,)),
            pltpu.SemaphoreType.REGULAR((2,)),
            dma((1,)),
            dma((1,)),
            dma((5,)),
            dma((2,)),
            dma((1,)),
        ],
        compiler_params=pltpu.CompilerParams(
            collective_id=0, has_side_effects=True, vmem_limit_bytes=40 * 1024 * 1024
        ),
        name="front",
    )(
        *(
            pltpu.with_memory_space_constraint(a, pltpu.HBM)
            for a in (
                activations,
                taps,
                patch_weight,
                patch_bias.reshape(1, -1),
                shift.reshape(1, -1),
                scale.reshape(1, -1),
                qkv,
                qkv_bias,
                norm_gains,
            )
        )
    )
    tokens = narrows * per
    return pl.pallas_call(
        back,
        out_shape=jax.ShapeDtypeStruct((3, 2 * tokens, 256), BF16),
        in_specs=[vmem] * 3,
        out_specs=any_spec,
        scratch_shapes=[
            pltpu.VMEM((2 * LANES, 768), BF16),
            pltpu.VMEM((3, 2 * tokens, 256), BF16),
            dma((1,)),
        ],
        compiler_params=pltpu.CompilerParams(vmem_limit_bytes=40 * 1024 * 1024),
        name="back",
    )(x, m, e)


def solution(mesh):
    placed = (
        P("wide", "narrow", None, None),
        P(),
        P(),
        P(),
        P(),
        P(),
        P("wide", None, "narrow"),
        P(None, "narrow"),
        P(),
    )
    return jax.shard_map(
        functools.partial(local, mesh.shape["wide"], mesh.shape["narrow"]),
        mesh=mesh,
        in_specs=placed,
        out_specs=P(None, "wide", "narrow"),
        check_vma=False,
    )
```
